32 devices in a mesh: seq: 8 (over z, y), head: 4 (over x, core).
Axes of the slice: x: 2, y: 2, z: 4, core: 2. Of those that a mesh axis runs over, the one named last changes fastest.
Arguments:
- query_input: bfloat16 [4096, 2048], P(('seq', 'head')), may hold values from -6 to 6
- key_input: bfloat16 [4096, 2048], P(('seq', 'head')), may hold values from -40 to 40
- value_input: bfloat16 [4096, 4096], P(('seq', 'head')), may hold values from -40 to 40
- gate_input: bfloat16 [4096, 4096], P(('seq', 'head')), may hold values from -6 to 6
- write_strength: bfloat16 [4096, 32], P(('seq', 'head')), may hold values from 0.0009 to 0.91
- log_decay: bfloat16 [4096, 32], P(('seq', 'head')), may hold values from -0.81 to 0
- filter_query: bfloat16 [4, 2048], P(None, 'head'), may hold values from -3 to 3
- filter_key: bfloat16 [4, 2048], P(None, 'head'), may hold values from -3 to 3
- filter_value: bfloat16 [4, 4096], P(None, 'head'), may hold values from -3 to 3
- norm_gain: float32 [128], replicated, may hold values from 0.1 to 1.9
- out_weight: bfloat16 [4096, 2048], P('head'), may hold values from -0.09375 to 0.09375
Outputs:
- stratum_result: bfloat16 [4096, 2048], P(('seq', 'head'))
The draws below stay inside these ranges and needn't reach their ends.
All inputs are finite; a program needn't handle non-finite values.
Results may differ from the reference program's by a relative error of at most 0.005.
Values may be sent and summed in bfloat16 or wider, within the bound.
No kernel may reach another device: no remote copies, remote signals or barrier semaphores. Data moves between devices by JAX's collectives and lax.ppermute only.
A program may use at most 128 MiB of HBM per device.

```python
import math
import jax
import jax.numpy as jnp
from jax import lax

D = 2048
HK = 16
HV = 32
DK = 128
DV = 128
KW = 4
CH = 64
TOK_DEV = 512
L = 4096


def scaled_field(base_key, row_count, column_count):
    parts = jax.random.split(base_key, 3)
    base = jnp.clip(jax.random.normal(parts[0], (row_count, column_count), jnp.float32), -4.0, 4.0)
    column_scale = jnp.exp(jax.random.uniform(parts[1], (column_count,), jnp.float32, 0.0, math.log(10.0))) / math.sqrt(10.0)
    row_scale = jnp.exp(jax.random.uniform(parts[2], (row_count, 1), jnp.float32, 0.0, math.log(10.0))) / math.sqrt(10.0)
    return base * column_scale * row_scale


def head_layout(base_key):
    parts = jax.random.split(jax.random.fold_in(base_key, 21), 8)
    fast_share = 0.5
    fast_heads = jax.random.uniform(parts[0], (HV,), jnp.float32) < fast_share
    fast_rate = jnp.exp(jax.random.uniform(parts[1], (HV,), jnp.float32, math.log(1.0 / 40.0), math.log(1.0 / 15.0)))
    slow_rate = jnp.exp(jax.random.uniform(parts[2], (HV,), jnp.float32, math.log(0.05), math.log(0.3))) / L
    head_decay_speed = jnp.where(fast_heads, fast_rate, slow_rate)
    block_count = L // TOK_DEV
    block_factor = jnp.exp(jax.random.uniform(parts[3], (block_count, 1, HV), jnp.float32, math.log(0.5), math.log(2.0)))
    token_factor = jax.random.uniform(parts[4], (block_count, TOK_DEV, HV), jnp.float32, 0.5, 1.5)
    forgetting_rates = -(head_decay_speed * block_factor * token_factor).reshape(L, HV)
    flagged_locations = jax.random.randint(parts[5], (2, HV), 0, L)
    sequence_offsets = jnp.arange(L, dtype=jnp.int32)[:, None]
    spike_clusters = (sequence_offsets == flagged_locations[0][None, :]) | (sequence_offsets == flagged_locations[1][None, :])
    error_measures = jax.random.uniform(parts[6], (L, HV), jnp.float32, math.log(0.55), math.log(0.8))
    forgetting_rates = forgetting_rates + jnp.where(spike_clusters, error_measures, 0.0)
    strong = jax.random.uniform(parts[7], (L, HV), jnp.float32, 0.3, 0.9)
    weak = jnp.exp(jax.random.uniform(jax.random.fold_in(parts[7], 1), (L, HV), jnp.float32, math.log(0.001), math.log(0.003)))
    strength = jnp.where(fast_heads[None, :], strong, weak)
    return (forgetting_rates, strength)


def draw_key_input(key, part):
    return scaled_field(jax.random.fold_in(key, 11), L, HK * DK).astype(jnp.bfloat16)


def draw_value_input(key, part):
    return scaled_field(jax.random.fold_in(key, 12), L, HV * DV).astype(jnp.bfloat16)


def draw_write_strength(key, part):
    forgetting_rates, strength = head_layout(key)
    return strength.astype(jnp.bfloat16)


def draw_log_decay(key, part):
    forgetting_rates, strength = head_layout(key)
    return forgetting_rates.astype(jnp.bfloat16)


def block_levels(rng, dims, cuts, smallest, largest):
    level = 1.0
    for dim, blocks in cuts:
        draws = jax.random.uniform(jax.random.fold_in(jax.random.fold_in(rng, 6), dim), (blocks,), jnp.float32, smallest / len(cuts), largest / len(cuts))
        level = level * jnp.repeat(jnp.exp(draws), dims[dim] // blocks).reshape((-1,) + (1,) * (len(dims) - 1 - dim))
    return level


def normal_values(stream_key, shape, width, most, shards=(), kind=jnp.bfloat16):
    array = jax.random.normal(stream_key, shape, jnp.float32) * width
    if len(shards) > 0:
        array = block_levels(stream_key, shape, shards, -0.22, 0.18) * array
    return jnp.clip(array, min=-most, max=most).astype(kind)


def setup_inputs(seed: int = 0) -> dict:
    key_list = jax.random.split(jax.random.key(seed), 12)
    return {
        "query_input": normal_values(key_list[0], (L, HK * DK), 1.0, 6.0, ((0, 32),)),
        "key_input": draw_key_input(jax.random.fold_in(key_list[11], 71), 0),
        "value_input": draw_value_input(jax.random.fold_in(key_list[11], 71), 0),
        "gate_input": normal_values(key_list[3], (L, HV * DV), 1.0, 6.0, ((0, 32),)),
        "write_strength": draw_write_strength(jax.random.fold_in(key_list[11], 71), 0),
        "log_decay": draw_log_decay(jax.random.fold_in(key_list[11], 71), 0),
        "filter_query": normal_values(key_list[6], (KW, HK * DK), 0.5, 3.0, ((1, 4),)),
        "filter_key": normal_values(key_list[7], (KW, HK * DK), 0.5, 3.0, ((1, 4),)),
        "filter_value": normal_values(key_list[8], (KW, HV * DV), 0.5, 3.0, ((1, 4),)),
        "norm_gain": jnp.clip(1.0 + 0.18 * jax.random.normal(key_list[9], (DV,), jnp.float32), 0.1, 1.9),
        "out_weight": normal_values(key_list[10], (HV * DV, D), (HV * DV) ** -0.5, 0.09375, ((0, 4),)),
    }


exact_mode = lax.Precision.HIGHEST
norm_floor = 1e-06

def stretch_terms(query_rows, unit_keys, values, strength, forgetting_rates):
    block_width = forgetting_rates.shape[-1]
    value_width = values.shape[-1]
    key_width = unit_keys.shape[-1]
    token_index = lax.broadcasted_iota(jnp.int32, (block_width, block_width), 0)
    column_index = lax.broadcasted_iota(jnp.int32, (block_width, block_width), 1)
    inclusive = (column_index <= token_index).astype(jnp.float32)
    strict = (column_index < token_index).astype(jnp.float32)
    cumulative = jnp.cumsum(forgetting_rates, axis=-1)
    spread = cumulative[..., :, None] - cumulative[..., None, :]
    ratios = jnp.exp(spread * inclusive) * inclusive
    key_key = jnp.einsum('...id,...jd->...ij', unit_keys, unit_keys, precision=exact_mode)
    query_key = jnp.einsum('...id,...jd->...ij', query_rows, unit_keys, precision=exact_mode)
    lower_part = strength[..., :, None] * key_key * ratios * strict
    query_mix = query_key * ratios
    growth = jnp.exp(cumulative)
    right_side = jnp.concatenate([strength[..., None] * values, (strength * growth)[..., None] * unit_keys], axis=-1)
    system = lower_part + jnp.eye(block_width, dtype=jnp.float32)
    solved = jax.scipy.linalg.solve_triangular(system, right_side, lower=True, unit_diagonal=True)
    written = solved[..., :value_width]
    erased = solved[..., value_width:]
    tail_decay = jnp.exp(cumulative[..., -1:] - cumulative)
    tailed = unit_keys * tail_decay[..., None]
    carry_map = jnp.exp(cumulative[..., -1])[..., None, None] * jnp.eye(key_width, dtype=jnp.float32) - jnp.einsum('...id,...ie->...de', tailed, erased, precision=exact_mode)
    carry_add = jnp.einsum('...id,...ie->...de', tailed, written, precision=exact_mode)
    local_out = jnp.einsum('...ij,...je->...ie', query_mix, written, precision=exact_mode)
    entry_map = growth[..., None] * query_rows - jnp.einsum('...ij,...jd->...id', query_mix, erased, precision=exact_mode)
    return (carry_map, carry_add, local_out, entry_map)

def causal_filter(signal, filter_taps):
    kernel_width = filter_taps.shape[0]
    length = signal.shape[0]
    padded = jnp.concatenate([jnp.zeros((kernel_width - 1, signal.shape[1]), jnp.float32), signal.astype(jnp.float32)], axis=0)
    summed = jnp.zeros(signal.shape, jnp.float32)
    for offset in range(kernel_width):
        summed = summed + filter_taps[offset].astype(jnp.float32) * padded[offset:offset + length]
    return jax.nn.silu(summed)

def unit_rows(field):
    return field / jnp.sqrt(lax.optimization_barrier(jnp.sum(field * field, axis=-1, keepdims=True)) + norm_floor)

def reference(query_input, key_input, value_input, gate_input, write_strength, log_decay, filter_query, filter_key, filter_value, norm_gain, out_weight):
    query_rows = unit_rows(causal_filter(query_input, filter_query).reshape(L, HK, DK)) * DK ** (-0.5)
    unit_keys = unit_rows(causal_filter(key_input, filter_key).reshape(L, HK, DK))
    values = causal_filter(value_input, filter_value).reshape(L, HV, DV)
    sharing = HV // HK
    blocks = L // CH

    def one_head(head_index):
        source = head_index // sharing
        head_query = lax.dynamic_index_in_dim(query_rows, source, 1, keepdims=False).reshape(blocks, CH, DK)
        head_key = lax.dynamic_index_in_dim(unit_keys, source, 1, keepdims=False).reshape(blocks, CH, DK)
        head_value = lax.dynamic_index_in_dim(values, head_index, 1, keepdims=False).reshape(blocks, CH, DV)
        strength = lax.dynamic_index_in_dim(write_strength, head_index, 1, keepdims=False).astype(jnp.float32).reshape(blocks, CH)
        forgetting_rates = lax.dynamic_index_in_dim(log_decay, head_index, 1, keepdims=False).astype(jnp.float32).reshape(blocks, CH)
        carry_map, carry_add, local_out, entry_map = stretch_terms(head_query, head_key, head_value, strength, forgetting_rates)

        def advance(running, pieces):
            block_map, block_add, block_out, block_entry = pieces
            emitted = block_out + jnp.dot(block_entry, running, precision=exact_mode)
            return (jnp.dot(block_map, running, precision=exact_mode) + block_add, emitted)
        final_state, outputs = lax.scan(advance, jnp.zeros((DK, DV), jnp.float32), (carry_map, carry_add, local_out, entry_map))
        return outputs.reshape(L, DV)
    core_out = lax.map(one_head, jnp.arange(HV, dtype=jnp.int32))
    core_out = jnp.transpose(core_out, (1, 0, 2))
    inverse_rms = lax.rsqrt(lax.optimization_barrier(jnp.mean(core_out * core_out, axis=-1, keepdims=True)) + norm_floor)
    gating = jax.nn.silu(gate_input.astype(jnp.float32)).reshape(L, HV, DV)
    normed = (core_out * inverse_rms * norm_gain * gating).astype(jnp.bfloat16).reshape(L, HV * DV)
    return jnp.dot(normed.astype(jnp.float32), out_weight.astype(jnp.float32), preferred_element_type=jnp.float32).astype(jnp.bfloat16)
```

```python
import functools

import jax
import jax.numpy as jnp
from jax import lax
from jax.experimental import pallas as pl
from jax.experimental.pallas import tpu as pltpu
from jax.sharding import PartitionSpec as P

HK = 16
HV = 32
DK = 128
DV = 128
CH = 128
EDGE = 16
SHARE = HV // HK

norm_floor = 1e-06
f32 = jnp.float32
bf16 = jnp.bfloat16


def params(megabytes=48):
    return pltpu.CompilerParams(vmem_limit_bytes=megabytes * 1024 * 1024)


def split(x):
    high = x.astype(bf16)
    return high, (x - high.astype(f32)).astype(bf16)


def as_left(x):
    return jnp.concatenate(split(x), axis=1)


def right_of(high, low):
    row = jnp.concatenate([high, low], axis=1)
    return jnp.concatenate([row, row], axis=0)


def as_right(x):
    return right_of(*split(x))


def product(left, right):
    both = jnp.dot(left, right, preferred_element_type=f32)
    half = both.shape[1] // 2
    return both[:, :half] + both[:, half:]


def grids():
    row = lax.broadcasted_iota(jnp.int32, (CH, CH), 0)
    column = lax.broadcasted_iota(jnp.int32, (CH, CH), 1)
    return row, column


def ones_where(mask):
    return jnp.where(mask, 1.0, 0.0).astype(bf16)


def conv_silu(rows_ref, edge_ref, taps_ref, padded):
    length = rows_ref.shape[0]
    taps = taps_ref[...].astype(f32)
    padded[0:8] = edge_ref[...].astype(f32)[EDGE - 8 : EDGE]
    padded[8 : 8 + length] = rows_ref[...].astype(f32)
    margin = taps.shape[0] - 1
    summed = taps[margin : margin + 1] * padded[8 : 8 + length]
    for offset in range(margin):
        start = 8 - margin + offset
        summed = summed + taps[offset : offset + 1] * padded[start : start + length]
    return summed / (1.0 + jnp.exp(-summed))


def unit_rows(field):
    return field * lax.rsqrt(jnp.sum(field * field, axis=-1, keepdims=True) + norm_floor)


def decay_terms(gates, head, value_heads):
    row, column = grids()
    pick_row = lax.broadcasted_iota(jnp.int32, (gates.shape[1], CH), 0)
    picks = jnp.concatenate(
        [ones_where(pick_row == head), ones_where(pick_row == value_heads + head)], axis=1
    )
    picked = jnp.dot(gates, picks, preferred_element_type=f32)
    strength = picked[:, :CH]
    rate = picked[:, CH:].astype(bf16)
    below = ones_where(column <= row)
    after = jnp.where(row > column, rate, jnp.zeros_like(rate))
    sums = jnp.dot(below, jnp.concatenate([after, rate], axis=1), preferred_element_type=f32)
    ratios = jnp.where(column <= row, jnp.exp(sums[:, :CH]), 0.0)
    growth = jnp.exp(sums[:, CH:])
    return strength, ratios, growth


def key_kernel(value_heads, rows, edge, taps, gates, t_out, kt_out, ktail_out, w_out, d_out, p_out, last_out, map_out, padded):
    kh = pl.program_id(0)
    blocks = rows.shape[0] // CH
    keys = unit_rows(conv_silu(rows, edge, taps, padded))
    row, column = grids()
    eye = jnp.where(row == column, 1.0, 0.0)
    strict = column < row
    problems = [(c, e) for c in range(blocks) for e in range(SHARE)]
    chunk = [keys[c * CH : (c + 1) * CH] for c in range(blocks)]
    turned = [jnp.transpose(x) for x in chunk]
    kk = [product(as_left(x), as_right(y)) for x, y in zip(chunk, turned)]
    for c in range(blocks):
        kt_out[0, c] = turned[c]
    lower, weights = {}, {}
    inverse = {}
    for c, e in problems:
        strength, ratios, growth = decay_terms(
            gates[c * CH : (c + 1) * CH, :], kh * SHARE + e, value_heads
        )
        system = jnp.where(strict, strength * kk[c] * ratios, 0.0)
        lower[c, e] = split(system)
        inverse[c, e] = eye - jnp.where((row // 2 == column // 2) & strict, system, 0.0)
        weights[c, e] = strength * growth * chunk[c]
        tail = as_left(turned[c] * ratios[CH - 1 : CH])
        ktail_out[0, c, e] = tail
        last_out[0, c, e] = growth[CH - 8 : CH]
        strength_row = jnp.dot(
            jnp.ones((8, CH), bf16),
            (strength * eye).astype(bf16),
            preferred_element_type=f32,
        )
        t_out[0, c, e] = jnp.broadcast_to(strength_row[0:1], (CH, CH)).astype(f32)
    size = 2
    while size < CH:
        mask = ones_where(
            (row // (2 * size) == column // (2 * size))
            & ((row // size) % 2 == 1)
            & ((column // size) % 2 == 0)
        )
        parts = {pc: split(inverse[pc]) for pc in problems}
        first = {
            pc: product(
                jnp.concatenate([lower[pc][0] * mask, lower[pc][1] * mask], axis=1),
                right_of(*parts[pc]),
            )
            for pc in problems
        }
        for pc in problems:
            inverse[pc] = inverse[pc] - product(
                jnp.concatenate(parts[pc], axis=1), as_right(first[pc])
            )
        size *= 2
    maps = {}
    for c, e in problems:
        solved = product(as_left(inverse[c, e]), as_right(weights[c, e]))
        w_out[0, c, e] = solved
        t_out[0, c, e] = inverse[c, e] * t_out[0, c, e]
        maps[c, e] = product(ktail_out[0, c, e], as_right(solved))
        d_out[0, c, e] = as_left(maps[c, e])
    for e in range(SHARE):
        running = last_out[0, 0, e][7:8] * eye - maps[0, e]
        for c in range(1, blocks):
            p_out[0, c - 1, e] = running
            running = last_out[0, c, e][7:8] * running - product(
                d_out[0, c, e], as_right(running)
            )
        map_out[e] = (eye - running).astype(bf16)


def value_kernel(rows, edge, taps, t_in, ktail, d_in, last, u_out, z_out, add_out, padded):
    blocks = rows.shape[0] // CH
    values = conv_silu(rows, edge, taps, padded)
    adds = {}
    for c in range(blocks):
        for e in range(SHARE):
            mine = values[c * CH : (c + 1) * CH, e * DV : (e + 1) * DV]
            written = product(as_left(t_in[0, c, e]), as_right(mine))
            u_out[0, c, e] = written
            adds[c, e] = product(ktail[0, c, e], as_right(written))
    running = [adds[0, e] for e in range(SHARE)]
    for c in range(1, blocks):
        for e in range(SHARE):
            z_out[0, c - 1, e] = running[e]
            running[e] = (
                last[0, c, e][7:8] * running[e]
                - product(d_in[0, c, e], as_right(running[e]))
                + adds[c, e]
            )
    for e in range(SHARE):
        add_out[e] = running[e].astype(bf16)


def query_kernel(value_heads, rows, edge, taps, gates, kt_in, w_in, p_in, u_in, z_in, f_out, g_out, padded):
    kh = pl.program_id(0)
    blocks = rows.shape[0] // CH
    queries = unit_rows(conv_silu(rows, edge, taps, padded)) * DK ** (-0.5)
    for c in range(blocks):
        mine = queries[c * CH : (c + 1) * CH]
        qk = product(as_left(mine), as_right(kt_in[0, c]))
        for e in range(SHARE):
            strength, ratios, growth = decay_terms(
                gates[c * CH : (c + 1) * CH, :], kh * SHARE + e, value_heads
            )
            mix = as_left(qk * ratios)
            entry = growth * mine - product(mix, as_right(w_in[0, c, e]))
            local = product(mix, as_right(u_in[0, c, e]))
            here = slice(c * CH, (c + 1) * CH)
            if c == 0:
                f_out[e, here] = as_left(entry)
                g_out[e, here] = local
            else:
                entry = as_left(entry)
                f_out[e, here] = as_left(product(entry, as_right(p_in[0, c - 1, e])))
                g_out[e, here] = local + product(entry, as_right(z_in[0, c - 1, e]))


def handoff_kernel(maps, adds, out):
    spans, heads = maps.shape[0], maps.shape[1]
    for h in range(heads):
        running = jnp.zeros(out.shape[2:], f32)
        for j in range(spans):
            out[j, h] = running.astype(bf16)
            if j + 1 < spans:
                high, low = split(running)
                erased = jnp.dot(maps[j, h], high, preferred_element_type=f32) + jnp.dot(
                    maps[j, h], low, preferred_element_type=f32
                )
                running = running - erased + adds[j, h].astype(f32)


def norm_kernel(order, f_in, g_in, state, gate, gain, out):
    heads = state.shape[0]
    for h in range(heads):
        both = jnp.concatenate([state[h], state[h]], axis=0)
        core = g_in[h] + jnp.dot(f_in[h], both, preferred_element_type=f32)
        scale = lax.rsqrt(jnp.mean(core * core, axis=-1, keepdims=True) + norm_floor)
        columns = slice(h * DV, (h + 1) * DV)
        gates = gate[:, columns].astype(f32)
        gates = gates / (1.0 + jnp.exp(-gates))
        out[0, :, columns] = (core * scale * gain[...] * gates).astype(bf16)


def shape(dims, kind):
    return jax.ShapeDtypeStruct(dims, kind)


def per_head(dims):
    return pl.BlockSpec((1,) + dims, lambda p: (p,) + (0,) * len(dims))


def columns_of(rows, width):
    return pl.BlockSpec((rows, width), lambda p: (0, p))


def key_terms(packed, edge, taps):
    tokens = packed.shape[0]
    key_heads = taps.shape[1] // DK
    blocks = tokens // CH
    sides = (blocks, SHARE, CH)
    return pl.pallas_call(
        functools.partial(key_kernel, key_heads * SHARE),
        grid=(key_heads,),
        in_specs=[
            columns_of(tokens, DK),
            columns_of(EDGE, DK),
            columns_of(taps.shape[0], DK),
            pl.BlockSpec((tokens, 128), lambda p: (0, key_heads)),
        ],
        out_specs=[
            per_head(sides + (CH,)),
            per_head((blocks, DK, CH)),
            per_head((blocks, SHARE, DK, 2 * CH)),
            per_head(sides + (DK,)),
            per_head((blocks, SHARE, DK, 2 * DK)),
            per_head((blocks - 1, SHARE, DK, DK)),
            per_head((blocks, SHARE, 8, CH)),
            pl.BlockSpec((SHARE, DK, DK), lambda p: (p, 0, 0)),
        ],
        out_shape=[
            shape((key_heads,) + sides + (CH,), f32),
            shape((key_heads, blocks, DK, CH), f32),
            shape((key_heads, blocks, SHARE, DK, 2 * CH), bf16),
            shape((key_heads,) + sides + (DK,), f32),
            shape((key_heads, blocks, SHARE, DK, 2 * DK), bf16),
            shape((key_heads, blocks - 1, SHARE, DK, DK), f32),
            shape((key_heads, blocks, SHARE, 8, CH), f32),
            shape((key_heads * SHARE, DK, DK), bf16),
        ],
        scratch_shapes=[pltpu.VMEM((tokens + 8, DK), f32)],
        compiler_params=params(),
        name="key_terms",
    )(packed, edge, taps, packed)


def value_terms(rows, edge, taps, t_in, ktail, d_in, last):
    tokens = rows.shape[0]
    key_heads = t_in.shape[0]
    blocks = tokens // CH
    width = SHARE * DV
    sides = (blocks, SHARE, CH)
    return pl.pallas_call(
        value_kernel,
        grid=(key_heads,),
        in_specs=[
            columns_of(tokens, width),
            columns_of(EDGE, width),
            columns_of(taps.shape[0], width),
            per_head(sides + (CH,)),
            per_head((blocks, SHARE, DK, 2 * CH)),
            per_head((blocks, SHARE, DK, 2 * DK)),
            per_head((blocks, SHARE, 8, CH)),
        ],
        out_specs=[
            per_head(sides + (DV,)),
            per_head((blocks - 1, SHARE, DK, DV)),
            pl.BlockSpec((SHARE, DK, DV), lambda p: (p, 0, 0)),
        ],
        out_shape=[
            shape((key_heads,) + sides + (DV,), f32),
            shape((key_heads, blocks - 1, SHARE, DK, DV), f32),
            shape((key_heads * SHARE, DK, DV), bf16),
        ],
        scratch_shapes=[pltpu.VMEM((tokens + 8, width), f32)],
        compiler_params=params(),
        name="value_terms",
    )(rows, edge, taps, t_in, ktail, d_in, last)


def query_terms(rows, edge, taps, packed, kt, w, p, u, z):
    tokens = rows.shape[0]
    key_heads = kt.shape[0]
    blocks = tokens // CH
    sides = (blocks, SHARE, CH)
    return pl.pallas_call(
        functools.partial(query_kernel, key_heads * SHARE),
        grid=(key_heads,),
        in_specs=[
            columns_of(tokens, DK),
            columns_of(EDGE, DK),
            columns_of(taps.shape[0], DK),
            pl.BlockSpec((tokens, 128), lambda p: (0, key_heads)),
            per_head((blocks, DK, CH)),
            per_head(sides + (DK,)),
            per_head((blocks - 1, SHARE, DK, DK)),
            per_head(sides + (DV,)),
            per_head((blocks - 1, SHARE, DK, DV)),
        ],
        out_specs=[
            pl.BlockSpec((SHARE, tokens, 2 * DK), lambda p: (p, 0, 0)),
            pl.BlockSpec((SHARE, tokens, DV), lambda p: (p, 0, 0)),
        ],
        out_shape=[
            shape((key_heads * SHARE, tokens, 2 * DK), bf16),
            shape((key_heads * SHARE, tokens, DV), f32),
        ],
        scratch_shapes=[pltpu.VMEM((tokens + 8, DK), f32)],
        compiler_params=params(),
        name="query_terms",
    )(rows, edge, taps, packed, kt, w, p, u, z)


def handoff(maps, adds):
    return pl.pallas_call(
        handoff_kernel,
        out_shape=shape(adds.shape, bf16),
        compiler_params=params(),
        name="handoff",
    )(maps, adds)


def normed_rows(order, f, g, state, gate, gain):
    heads, tokens = g.shape[0], g.shape[1]
    own = order.shape[0]
    size = tokens // (2 * own)
    return pl.pallas_call(
        norm_kernel,
        grid_spec=pltpu.PrefetchScalarGridSpec(
            num_scalar_prefetch=1,
            grid=(own,),
            in_specs=[
                pl.BlockSpec((heads, size, 2 * DK), lambda i, order: (0, order[i], 0)),
                pl.BlockSpec((heads, size, DV), lambda i, order: (0, order[i], 0)),
                pl.BlockSpec((heads, DK, DV), lambda i, order: (0, 0, 0)),
                pl.BlockSpec((size, heads * DV), lambda i, order: (order[i], 0)),
                pl.BlockSpec((1, DV), lambda i, order: (0, 0)),
            ],
            out_specs=pl.BlockSpec((1, size, heads * DV), lambda i, order: (i, 0, 0)),
        ),
        out_shape=shape((own, size, heads * DV), bf16),
        compiler_params=params(),
        name="normed_rows",
    )(order, f, g, state, gate, gain)


def by_group(rows, groups):
    return rows.reshape(rows.shape[0], groups, rows.shape[1] // groups).transpose(1, 0, 2)


def spread(pieces):
    got = lax.all_to_all(pieces, "head", 0, 0)
    return got.reshape(got.shape[0] * got.shape[1], got.shape[2])


def entry_states(maps, adds):
    spans = lax.axis_size("seq")
    heads = maps.shape[0]
    each = max(1, heads // spans)
    cuts = max(1, spans // heads)
    width = DV // cuts
    maps = maps.reshape(heads // each, each, DK, DK)
    maps = jnp.repeat(maps, cuts, axis=0) if cuts > 1 else maps
    adds = adds.reshape(heads // each, each, DK, cuts, width)
    adds = adds.transpose(0, 3, 1, 2, 4).reshape(spans, each, DK, width)
    maps = lax.all_to_all(maps, "seq", 0, 0)
    adds = lax.all_to_all(adds, "seq", 0, 0)
    entries = lax.all_to_all(handoff(maps, adds), "seq", 0, 0)
    entries = entries.reshape(heads // each, cuts, each, DK, width)
    return entries.transpose(0, 2, 3, 1, 4).reshape(heads, DK, DV)


def on_device(
    query_input,
    key_input,
    value_input,
    gate_input,
    write_strength,
    log_decay,
    filter_query,
    filter_key,
    filter_value,
    norm_gain,
    out_weight,
):
    groups = lax.axis_size("head")
    spans = lax.axis_size("seq")
    member = lax.axis_index("head")
    own_tokens = query_input.shape[0]

    edges = jnp.concatenate(
        [by_group(x[-EDGE:], groups) for x in (query_input, key_input, value_input)], axis=2
    )
    edge = None
    for h in range(groups):
        pairs = [(s * groups + groups - 1, (s + 1) * groups + h) for s in range(spans - 1)]
        moved = lax.ppermute(edges[h], ("seq", "head"), pairs)
        edge = moved if edge is None else edge + moved
    key_width = filter_key.shape[1]
    query_edge = edge[:, :key_width]
    key_edge = edge[:, key_width : 2 * key_width]
    value_edge = edge[:, 2 * key_width :]

    gates = jnp.concatenate(
        [by_group(write_strength, groups), by_group(log_decay, groups)], axis=2
    )
    gates = jnp.pad(gates, ((0, 0), (0, 0), (0, 128 - gates.shape[2])))
    packed = spread(jnp.concatenate([by_group(key_input, groups), gates], axis=2))
    value_rows = spread(by_group(value_input, groups))
    query_rows = spread(by_group(query_input, groups))
    gate_rows = spread(by_group(gate_input, groups))

    t, kt, ktail, w, d, p, last, maps = key_terms(packed, key_edge, filter_key)
    u, z, adds = value_terms(value_rows, value_edge, filter_value, t, ktail, d, last)
    f, g = query_terms(query_rows, query_edge, filter_query, packed, kt, w, p, u, z)
    state = entry_states(maps, adds)

    side = member % 2
    rank = member // 2
    ranks = groups // 2
    near = jnp.arange(ranks, dtype=jnp.int32) ^ rank
    gain = norm_gain.reshape(1, DV)
    swap = [(i, i ^ 1) for i in range(groups)]
    other_weight = lax.ppermute(out_weight, "head", swap)
    theirs = normed_rows(2 * near + 1 - side, f, g, state, gate_rows, gain)
    theirs = lax.ppermute(theirs, "head", swap)
    mine = normed_rows(2 * near + side, f, g, state, gate_rows, gain)
    total = None
    for step in range(ranks - 1, -1, -1):
        part = jnp.dot(mine[step], out_weight, preferred_element_type=f32) + jnp.dot(
            theirs[step], other_weight, preferred_element_type=f32
        )
        if step > 0:
            part = lax.ppermute(
                part.astype(bf16), "head", [(i, i ^ (2 * step)) for i in range(groups)]
            ).astype(f32)
        total = part if total is None else total + part
    return total.astype(bf16)


def solution(mesh):
    tokens = P(("seq", "head"), None)
    placed = (tokens,) * 6 + (P(None, "head"),) * 3 + (P(), P("head", None))
    return jax.shard_map(
        on_device, mesh=mesh, in_specs=placed, out_specs=tokens, check_vma=False
    )
```

```python
import functools

import jax
import jax.numpy as jnp
from jax import lax
from jax.experimental import pallas as pl
from jax.experimental.pallas import tpu as pltpu
from jax.sharding import PartitionSpec as P

HK = 16
HV = 32
DK = 128
DV = 128
CH = 128
EDGE = 16
SHARE = HV // HK

norm_floor = 1e-06
f32 = jnp.float32
bf16 = jnp.bfloat16


def params(megabytes=60):
    return pltpu.CompilerParams(vmem_limit_bytes=megabytes * 1024 * 1024)


def split(x):
    high = x.astype(bf16)
    return high, (x - high.astype(f32)).astype(bf16)


def as_left(x):
    return jnp.concatenate(split(x), axis=1)


def right_of(high, low):
    row = jnp.concatenate([high, low], axis=1)
    return jnp.concatenate([row, row], axis=0)


def as_right(x):
    return right_of(*split(x))


def product(left, right):
    both = jnp.dot(left, right, preferred_element_type=f32)
    half = both.shape[1] // 2
    return both[:, :half] + both[:, half:]


def grids():
    row = lax.broadcasted_iota(jnp.int32, (CH, CH), 0)
    column = lax.broadcasted_iota(jnp.int32, (CH, CH), 1)
    return row, column


def ones_where(mask):
    return jnp.where(mask, 1.0, 0.0).astype(bf16)


def place(me, pieces, out, margin):
    size = pieces[0].shape[0]
    for d, piece in enumerate(pieces):
        at = pl.multiple_of((me ^ d) * size + margin, 8)
        out[pl.ds(at, size), :] = piece[...].astype(out.dtype)


def conv_silu(me, pieces, edges, taps_ref, padded):
    length = padded.shape[0] - 8
    taps = taps_ref[...].astype(f32)
    edge = edges[0][...].astype(f32)
    for other in edges[1:]:
        edge = edge + other[...].astype(f32)
    padded[0:8] = edge[EDGE - 8 : EDGE]
    place(me, pieces, padded, 8)
    margin = taps.shape[0] - 1
    summed = taps[margin : margin + 1] * padded[8 : 8 + length]
    for offset in range(margin):
        start = 8 - margin + offset
        summed = summed + taps[offset : offset + 1] * padded[start : start + length]
    return summed / (1.0 + jnp.exp(-summed))


def unit_rows(field):
    return field * lax.rsqrt(jnp.sum(field * field, axis=-1, keepdims=True) + norm_floor)


def strengths_and_rates(gates, first, count):
    lane = lax.broadcasted_iota(jnp.int32, (gates.shape[1], CH), 0)
    picks = [ones_where(lane == first + e) for e in range(count)]
    picks += [ones_where(lane == HV + first + e) for e in range(count)]
    picked = jnp.dot(gates, jnp.concatenate(picks, axis=1), preferred_element_type=f32)
    return picked[:, : count * CH], picked[:, count * CH :].astype(bf16)


def decay_terms(rates, count):
    row, column = grids()
    below = ones_where(column <= row)
    pieces = []
    for e in range(count):
        rate = rates[:, e * CH : (e + 1) * CH]
        pieces += [jnp.where(row > column, rate, jnp.zeros_like(rate)), rate]
    sums = jnp.dot(below, jnp.concatenate(pieces, axis=1), preferred_element_type=f32)
    ratios, growth = [], []
    for e in range(count):
        at = 2 * e * CH
        ratios.append(jnp.where(column <= row, jnp.exp(sums[:, at : at + CH]), 0.0))
        growth.append(jnp.exp(sums[:, at + CH : at + 2 * CH]))
    return ratios, growth


def unit_lower_inverses(lower):
    row, column = grids()
    names = list(lower)
    eye = jnp.where(row == column, 1.0, 0.0)
    pair = (row // 2 == column // 2) & (column < row)
    halves = {n: split(lower[n]) for n in names}
    inverse = {n: eye - jnp.where(pair, lower[n], 0.0) for n in names}
    size = 2
    while size < CH:
        mask = ones_where(
            (row // (2 * size) == column // (2 * size))
            & ((row // size) % 2 == 1)
            & ((column // size) % 2 == 0)
        )
        rounded = {n: inverse[n].astype(bf16) for n in names}
        first = {
            n: jnp.dot(halves[n][0] * mask, rounded[n], preferred_element_type=f32).astype(bf16)
            for n in names
        }
        for n in names:
            inverse[n] = inverse[n] - jnp.dot(rounded[n], first[n], preferred_element_type=f32)
        size *= 2
    parts = {n: split(inverse[n]) for n in names}
    left = {
        n: (
            eye
            - inverse[n]
            - product(jnp.concatenate(halves[n], axis=1), right_of(*parts[n]))
        ).astype(bf16)
        for n in names
    }
    return {
        n: inverse[n] + jnp.dot(parts[n][0], left[n], preferred_element_type=f32) for n in names
    }


def key_kernel(groups_count, heads, member, *refs):
    pieces, refs = refs[:groups_count], refs[groups_count:]
    edges, refs = refs[:groups_count], refs[groups_count:]
    gate_pieces, refs = refs[:groups_count], refs[groups_count:]
    taps, t_out, kt_out, ktail_out, w_out, d_out, p_out, last_out, map_out, padded, gates = refs
    here = pieces[0].shape[1] // DK
    count = here * SHARE
    blocks = gates.shape[0] // CH
    me = member[0]
    first = me * heads + pl.program_id(0) * count
    filtered = conv_silu(me, pieces, edges, taps, padded)
    place(me, gate_pieces, gates, 0)
    row, column = grids()
    eye = jnp.where(row == column, 1.0, 0.0)
    groups = [(c, k) for c in range(blocks) for k in range(here)]
    problems = [(c, e) for c in range(blocks) for e in range(count)]

    def chunk_of(x, c):
        return x[c * CH : (c + 1) * CH]

    strengths, rates = strengths_and_rates(gates[...], first, count)
    unit = [unit_rows(filtered[:, k * DK : (k + 1) * DK]) for k in range(here)]
    decays = [decay_terms(chunk_of(rates, c), count) for c in range(blocks)]
    keys = {(c, k): chunk_of(unit[k], c) for c, k in groups}
    turned = {g: jnp.transpose(keys[g]) for g in groups}
    sides = {g: split(turned[g]) for g in groups}
    kk = {g: product(as_left(keys[g]), right_of(*sides[g])) for g in groups}
    lane = lax.broadcasted_iota(jnp.int32, (8, gates.shape[1]), 1)
    order = lax.broadcasted_iota(jnp.int32, (8, gates.shape[1]), 0)
    pick = ones_where(lane == first + order)
    across = [
        lax.dot_general(
            pick,
            gates[c * CH : (c + 1) * CH, :],
            (((1,), (1,)), ((), ())),
            preferred_element_type=f32,
        )
        for c in range(blocks)
    ]
    lower, ktail = {}, {}
    for c, k in groups:
        kt_out[k, c] = jnp.concatenate(sides[c, k], axis=1)
    for c, e in problems:
        ratios, growth = decays[c][0][e], decays[c][1][e]
        strength = chunk_of(strengths, c)[:, e * CH : (e + 1) * CH]
        k = e // SHARE
        lower[c, e] = jnp.where(column < row, strength * kk[c, k] * ratios, 0.0)
        ktail[c, e] = as_left(turned[c, k] * ratios[CH - 1 : CH])
        ktail_out[k, c, e % SHARE] = ktail[c, e]
        last_out[k, c, e % SHARE] = growth[CH - 8 : CH]
    inverse = unit_lower_inverses(lower)
    solving = {(c, e): as_left(inverse[c, e] * across[c][e : e + 1]) for c, e in problems}
    solved = {
        (c, e): product(solving[c, e], as_right(decays[c][1][e] * keys[c, e // SHARE]))
        for c, e in problems
    }
    erasing = {pc: split(solved[pc]) for pc in problems}
    maps = {pc: as_left(product(ktail[pc], right_of(*erasing[pc]))) for pc in problems}
    for c, e in problems:
        k = e // SHARE
        t_out[k, c, e % SHARE] = solving[c, e]
        w_out[k, c, e % SHARE] = jnp.concatenate(erasing[c, e], axis=1)
        d_out[k, c, e % SHARE] = maps[c, e]
    running = []
    for e in range(count):
        high, low = maps[0, e][:, :DK], maps[0, e][:, DK:]
        running.append(
            decays[0][1][e][CH - 1 : CH] * eye - (high.astype(f32) + low.astype(f32))
        )
    for c in range(1, blocks):
        parts = [split(x) for x in running]
        for e in range(count):
            p_out[e // SHARE, c - 1, e % SHARE] = jnp.concatenate(parts[e], axis=1)
        running = [
            decays[c][1][e][CH - 1 : CH] * running[e] - product(maps[c, e], right_of(*parts[e]))
            for e in range(count)
        ]
    for e in range(count):
        map_out[e] = (eye - running[e]).astype(bf16)


def right_from(both):
    return jnp.concatenate([both, both], axis=0)


def value_kernel(groups_count, member, *refs):
    pieces, refs = refs[:groups_count], refs[groups_count:]
    edges, refs = refs[:groups_count], refs[groups_count:]
    taps, t_in, ktail, d_in, last, u_out, z_out, add_out, padded = refs
    blocks = t_in.shape[1]
    count = pieces[0].shape[1] // DV
    values = conv_silu(member[0], pieces, edges, taps, padded)
    problems = [(c, e) for c in range(blocks) for e in range(count)]

    def at(ref, c, e):
        return ref[e // SHARE, c, e % SHARE]

    written = {
        (c, e): split(
            product(
                at(t_in, c, e),
                as_right(values[c * CH : (c + 1) * CH, e * DV : (e + 1) * DV]),
            )
        )
        for c, e in problems
    }
    adds = {pc: product(at(ktail, *pc), right_of(*written[pc])) for pc in problems}
    for c, e in problems:
        u_out[e // SHARE, c, e % SHARE] = jnp.concatenate(written[c, e], axis=1)
    running = [adds[0, e] for e in range(count)]
    for c in range(1, blocks):
        parts = [split(x) for x in running]
        for e in range(count):
            z_out[e // SHARE, c - 1, e % SHARE] = jnp.concatenate(parts[e], axis=1)
        running = [
            at(last, c, e)[7:8] * running[e]
            - product(at(d_in, c, e), right_of(*parts[e]))
            + adds[c, e]
            for e in range(count)
        ]
    for e in range(count):
        add_out[e] = running[e].astype(bf16)


def query_kernel(groups_count, heads, member, *refs):
    pieces, refs = refs[:groups_count], refs[groups_count:]
    edges, refs = refs[:groups_count], refs[groups_count:]
    gate_pieces, refs = refs[:groups_count], refs[groups_count:]
    taps, kt_in, w_in, p_in, u_in, z_in, f_out, g_out, padded, gates = refs
    here = pieces[0].shape[1] // DK
    count = here * SHARE
    blocks = gates.shape[0] // CH
    me = member[0]
    first = me * heads + pl.program_id(0) * count
    filtered = conv_silu(me, pieces, edges, taps, padded)
    place(me, gate_pieces, gates, 0)
    unit = [unit_rows(filtered[:, k * DK : (k + 1) * DK]) * DK ** (-0.5) for k in range(here)]
    problems = [(c, e) for c in range(blocks) for e in range(count)]
    strengths, rates = strengths_and_rates(gates[...], first, count)
    decays = [decay_terms(rates[c * CH : (c + 1) * CH], count) for c in range(blocks)]

    def at(ref, c, e):
        return right_from(ref[e // SHARE, c, e % SHARE])

    queries = {
        (c, k): unit[k][c * CH : (c + 1) * CH] for c in range(blocks) for k in range(here)
    }
    qk = {
        (c, k): product(as_left(queries[c, k]), right_from(kt_in[k, c])) for c, k in queries
    }
    mix = {(c, e): as_left(qk[c, e // SHARE] * decays[c][0][e]) for c, e in problems}
    entry = {
        (c, e): as_left(
            decays[c][1][e] * queries[c, e // SHARE] - product(mix[c, e], at(w_in, c, e))
        )
        for c, e in problems
    }
    local = {pc: product(mix[pc], at(u_in, *pc)) for pc in problems}
    for c, e in problems:
        here = slice(c * CH, (c + 1) * CH)
        if c == 0:
            f_out[e, here] = entry[c, e]
            g_out[e, here] = local[c, e]
        else:
            f_out[e, here] = as_left(product(entry[c, e], at(p_in, c - 1, e)))
            g_out[e, here] = local[c, e] + product(entry[c, e], at(z_in, c - 1, e))


def handoff_kernel(maps, adds, out):
    spans, heads = maps.shape[0], maps.shape[1]
    width = out.shape[3]
    running = [jnp.zeros(out.shape[2:], f32) for h in range(heads)]
    for j in range(spans):
        for h in range(heads):
            out[j, h] = running[h].astype(bf16)
        if j + 1 < spans:
            for h in range(heads):
                high, low = split(running[h])
                both = jnp.concatenate([high, low], axis=1) if width % 128 == 0 else None
                if both is None:
                    erased = jnp.dot(maps[j, h], high, preferred_element_type=f32)
                    erased = erased + jnp.dot(maps[j, h], low, preferred_element_type=f32)
                else:
                    erased = jnp.dot(maps[j, h], both, preferred_element_type=f32)
                    erased = erased[:, :width] + erased[:, width:]
                running[h] = running[h] - erased + adds[j, h].astype(f32)


def norm_kernel(count, member, *refs):
    f_in, refs = refs[:count], refs[count:]
    g_in, refs = refs[:count], refs[count:]
    gate, refs = refs[:count], refs[count:]
    state, gain, out = refs
    heads = state.shape[0]
    cells = [(i, h) for i in range(count) for h in range(heads)]
    states = [jnp.concatenate([state[h], state[h]], axis=0) for h in range(heads)]
    core = {
        (i, h): g_in[i][h] + jnp.dot(f_in[i][h], states[h], preferred_element_type=f32)
        for i, h in cells
    }
    scale = {
        n: lax.rsqrt(jnp.mean(core[n] * core[n], axis=-1, keepdims=True) + norm_floor)
        for n in cells
    }
    for i, h in cells:
        columns = slice(h * DV, (h + 1) * DV)
        gates = gate[i][:, columns].astype(f32)
        gates = gates / (1.0 + jnp.exp(-gates))
        out[i, :, columns] = (core[i, h] * scale[i, h] * gain[...] * gates).astype(bf16)


def project_kernel(mine, theirs, own_weight, other_weight, kept, *sent):
    rows, depth = mine.shape[0] * mine.shape[1], mine.shape[2]
    product_ = jnp.dot(
        mine[...].reshape(rows, depth), own_weight[...], preferred_element_type=f32
    ) + jnp.dot(theirs[...].reshape(rows, depth), other_weight[...], preferred_element_type=f32)
    size = mine.shape[1]
    kept[...] = product_[:size]
    for i, out in enumerate(sent):
        out[...] = product_[(i + 1) * size : (i + 2) * size].astype(bf16)


def pack_kernel(groups_count, member, *refs):
    array, outs = refs[0], refs[1:]
    me = member[0]
    width = array.shape[1] // groups_count
    for d in range(groups_count):
        at = pl.multiple_of((me ^ d) * width, 128)
        outs[d][...] = array[:, pl.ds(at, width)]


def pack_keys_kernel(groups_count, member, *refs):
    key, value_end, key_end, query_end, strength, decay = refs[:6]
    outs, edges = refs[6 : 6 + groups_count], refs[6 + groups_count :]
    me = member[0]
    width = key.shape[1] // groups_count
    for d in range(groups_count):
        at = pl.multiple_of((me ^ d) * width, 128)
        outs[d][:, :width] = key[:, pl.ds(at, width)]
        outs[d][:, width:] = jnp.zeros((key.shape[0], 128), bf16)
        outs[d][:, width : width + HV] = strength[...]
        outs[d][:, width + HV : width + 2 * HV] = decay[...]
    for h in range(groups_count):
        start = 0
        for array in (value_end, key_end, query_end):
            width = array.shape[1] // groups_count
            edges[h][:, start : start + width] = array[:, h * width : (h + 1) * width]
            start += width


def shape(dims, kind):
    return jax.ShapeDtypeStruct(dims, kind)


def pack(member, array, groups):
    tokens, width = array.shape[0], array.shape[1] // groups
    return pl.pallas_call(
        functools.partial(pack_kernel, groups),
        grid_spec=grid_of(
            1,
            [pl.BlockSpec(array.shape, lambda p, me: (0, 0))],
            [pl.BlockSpec((tokens, width), lambda p, me: (0, 0))] * groups,
            [],
        ),
        out_shape=[shape((tokens, width), bf16)] * groups,
        compiler_params=params(),
        name="pack",
    )(member, array)


def pack_keys(member, key, value, query, strength, decay, groups):
    tokens, width = key.shape[0], key.shape[1] // groups
    edge = (EDGE, sum(x.shape[1] for x in (value, key, query)) // groups)

    def whole(dims):
        return pl.BlockSpec(dims, lambda p, me: (0, 0))

    def end(x):
        return pl.BlockSpec((EDGE, x.shape[1]), lambda p, me: (tokens // EDGE - 1, 0))

    outs = pl.pallas_call(
        functools.partial(pack_keys_kernel, groups),
        grid_spec=grid_of(
            1,
            [whole(key.shape), end(value), end(key), end(query)]
            + [whole(strength.shape), whole(decay.shape)],
            [whole((tokens, width + 128))] * groups + [whole(edge)] * groups,
            [],
        ),
        out_shape=[shape((tokens, width + 128), bf16)] * groups + [shape(edge, bf16)] * groups,
        compiler_params=params(),
        name="pack_keys",
    )(member, key, value, key, query, strength, decay)
    return outs[:groups], outs[groups:]


def per_head(each, dims):
    return pl.BlockSpec((each,) + dims, lambda p, me: (p,) + (0,) * len(dims))


def columns_of(rows, width, skip=0):
    return pl.BlockSpec((rows, width), lambda p, me: (0, p + skip))


def heads_at_once(key_heads):
    return 2 if key_heads % 2 == 0 else 1


def cost(microseconds):
    return pl.CostEstimate(
        flops=int(microseconds * 1e9), bytes_accessed=int(microseconds * 3e6), transcendentals=0
    )


def grid_of(steps, in_specs, out_specs, scratch):
    return pltpu.PrefetchScalarGridSpec(
        num_scalar_prefetch=1,
        grid=(steps,),
        in_specs=in_specs,
        out_specs=out_specs,
        scratch_shapes=scratch,
    )


def key_terms(member, packed, edges, taps):
    groups = len(packed)
    own = packed[0].shape[0]
    tokens = groups * own
    key_heads = taps.shape[1] // DK
    each = heads_at_once(key_heads)
    blocks = tokens // CH
    wide = (blocks, SHARE, CH, 2 * CH)
    kinds = [
        wide,
        (blocks, DK, 2 * CH),
        wide,
        wide,
        wide,
        (blocks - 1, SHARE, DK, 2 * DK),
        (blocks, SHARE, 8, CH),
    ]
    types = [bf16] * 6 + [f32]
    return pl.pallas_call(
        functools.partial(key_kernel, groups, key_heads * SHARE),
        grid_spec=grid_of(
            key_heads // each,
            [columns_of(own, each * DK)] * groups
            + [columns_of(EDGE, each * DK, key_heads * SHARE // each)] * groups
            + [pl.BlockSpec((own, 128), lambda p, me: (0, key_heads))] * groups
            + [columns_of(taps.shape[0], each * DK)],
            [per_head(each, kind) for kind in kinds]
            + [pl.BlockSpec((each * SHARE, DK, DK), lambda p, me: (p, 0, 0))],
            [pltpu.VMEM((tokens + 8, each * DK), f32), pltpu.VMEM((tokens, 128), bf16)],
        ),
        out_shape=[shape((key_heads,) + kind, t) for kind, t in zip(kinds, types)]
        + [shape((key_heads * SHARE, DK, DK), bf16)],
        compiler_params=params(),
        cost_estimate=cost(12),
        name="key_terms",
    )(member, *packed, *edges, *packed, taps)


def value_terms(member, pieces, edges, taps, t_in, ktail, d_in, last):
    groups = len(pieces)
    own = pieces[0].shape[0]
    tokens = groups * own
    key_heads = t_in.shape[0]
    each = heads_at_once(key_heads)
    blocks = tokens // CH
    width = each * SHARE * DV
    return pl.pallas_call(
        functools.partial(value_kernel, groups),
        grid_spec=grid_of(
            key_heads // each,
            [columns_of(own, width)] * groups
            + [columns_of(EDGE, width)] * groups
            + [columns_of(taps.shape[0], width)]
            + [per_head(each, x.shape[1:]) for x in (t_in, ktail, d_in, last)],
            [
                per_head(each, (blocks, SHARE, CH, 2 * DV)),
                per_head(each, (blocks - 1, SHARE, DK, 2 * DV)),
                pl.BlockSpec((each * SHARE, DK, DV), lambda p, me: (p, 0, 0)),
            ],
            [pltpu.VMEM((tokens + 8, width), f32)],
        ),
        out_shape=[
            shape((key_heads, blocks, SHARE, CH, 2 * DV), bf16),
            shape((key_heads, blocks - 1, SHARE, DK, 2 * DV), bf16),
            shape((key_heads * SHARE, DK, DV), bf16),
        ],
        compiler_params=params(),
        cost_estimate=cost(7),
        name="value_terms",
    )(member, *pieces, *edges, taps, t_in, ktail, d_in, last)


def query_terms(member, pieces, edges, packed, taps, kt, w, p, u, z):
    groups = len(pieces)
    own = pieces[0].shape[0]
    tokens = groups * own
    key_heads = kt.shape[0]
    each = heads_at_once(key_heads)
    skip = (key_heads + key_heads * SHARE) // each
    return pl.pallas_call(
        functools.partial(query_kernel, groups, key_heads * SHARE),
        grid_spec=grid_of(
            key_heads // each,
            [columns_of(own, each * DK)] * groups
            + [columns_of(EDGE, each * DK, skip)] * groups
            + [pl.BlockSpec((own, 128), lambda p, me: (0, key_heads))] * groups
            + [columns_of(taps.shape[0], each * DK)]
            + [per_head(each, x.shape[1:]) for x in (kt, w, p, u, z)],
            [
                pl.BlockSpec((each * SHARE, tokens, 2 * DK), lambda p, me: (p, 0, 0)),
                pl.BlockSpec((each * SHARE, tokens, DV), lambda p, me: (p, 0, 0)),
            ],
            [pltpu.VMEM((tokens + 8, each * DK), f32), pltpu.VMEM((tokens, 128), bf16)],
        ),
        out_shape=[
            shape((key_heads * SHARE, tokens, 2 * DK), bf16),
            shape((key_heads * SHARE, tokens, DV), f32),
        ],
        compiler_params=params(),
        cost_estimate=cost(8),
        name="query_terms",
    )(member, *pieces, *edges, *packed, taps, kt, w, p, u, z)


def handoff(maps, adds):
    return pl.pallas_call(
        handoff_kernel,
        out_shape=shape(adds.shape, bf16),
        compiler_params=params(),
        cost_estimate=cost(3),
        name="handoff",
    )(maps, adds)


def normed_rows(member, f, g, state, gate, gain, parity):
    heads = g.shape[0]
    count = len(gate)
    size, width = gate[0].shape

    def token_block(i, depth):
        return pl.BlockSpec(
            (heads, size, depth), lambda p, me: (0, me[0] ^ (2 * i + parity), 0)
        )

    whole = pl.BlockSpec((size, width), lambda p, me: (0, 0))
    return pl.pallas_call(
        functools.partial(norm_kernel, count),
        grid_spec=grid_of(
            1,
            [token_block(i, 2 * DK) for i in range(count)]
            + [token_block(i, DV) for i in range(count)]
            + [whole] * count
            + [
                pl.BlockSpec((heads, DK, DV), lambda p, me: (0, 0, 0)),
                pl.BlockSpec((1, DV), lambda p, me: (0, 0)),
            ],
            pl.BlockSpec((count, size, width), lambda p, me: (0, 0, 0)),
            [],
        ),
        out_shape=shape((count, size, width), bf16),
        compiler_params=params(),
        cost_estimate=cost(3),
        name="normed_rows",
    )(member, *([f] * count), *([g] * count), *gate, state, gain)


def projected(mine, theirs, own_weight, other_weight, start, width):
    ranks, size, depth = mine.shape
    tile = min(width, 512)
    whole = pl.BlockSpec((ranks, size, depth), lambda j: (0, 0, 0))
    weight = pl.BlockSpec((depth, tile), lambda j: (0, j + start // tile))
    out = pl.BlockSpec((size, tile), lambda j: (0, j))
    return pl.pallas_call(
        project_kernel,
        grid=(width // tile,),
        in_specs=[whole, whole, weight, weight],
        out_specs=[out] * ranks,
        out_shape=[shape((size, width), f32)] + [shape((size, width), bf16)] * (ranks - 1),
        compiler_params=params(),
        cost_estimate=cost(3),
        name="projected",
    )(mine, theirs, own_weight, other_weight)


def to_members(pieces):
    groups = len(pieces)
    return [pieces[0]] + [
        lax.ppermute(pieces[d], "head", [(i, i ^ d) for i in range(groups)])
        for d in range(1, groups)
    ]


def after_all(values, others):
    return lax.optimization_barrier((*values, *others))[: len(values)]


def to_runners(maps):
    spans = lax.axis_size("seq")
    heads = maps.shape[0]
    each = max(1, heads // spans)
    maps = maps.reshape(heads // each, each, DK, DK)
    if spans > heads:
        maps = jnp.repeat(maps, spans // heads, axis=0)
    return lax.all_to_all(maps, "seq", 0, 0)


def columns_to_runners(adds):
    spans = lax.axis_size("seq")
    heads = adds.shape[0]
    each = max(1, heads // spans)
    cuts = max(1, spans // heads)
    adds = adds.reshape(heads // each, each, DK, cuts, DV // cuts)
    adds = adds.transpose(0, 3, 1, 2, 4).reshape(spans, each, DK, DV // cuts)
    return lax.all_to_all(adds, "seq", 0, 0)


def from_runners(entries, heads):
    spans, each, depth, width = entries.shape
    entries = lax.all_to_all(entries, "seq", 0, 0)
    entries = entries.reshape(heads // each, DV // width, each, depth, width)
    return entries.transpose(0, 2, 3, 1, 4).reshape(heads, depth, DV)


def on_device(
    query_input,
    key_input,
    value_input,
    gate_input,
    write_strength,
    log_decay,
    filter_query,
    filter_key,
    filter_value,
    norm_gain,
    out_weight,
):
    groups = lax.axis_size("head")
    spans = lax.axis_size("seq")
    member = lax.axis_index("head").astype(jnp.int32).reshape(1)
    heads = filter_value.shape[1] // DV

    key_out, edges = pack_keys(
        member, key_input, value_input, query_input, write_strength, log_decay, groups
    )
    edges = [
        lax.ppermute(
            edges[h],
            ("seq", "head"),
            [(s * groups + groups - 1, (s + 1) * groups + h) for s in range(spans - 1)],
        )
        for h in range(groups)
    ]
    packed = to_members(key_out)
    value_rows = to_members(after_all(pack(member, value_input, groups), packed))
    query_rows = to_members(after_all(pack(member, query_input, groups), value_rows))
    gate_rows = to_members(after_all(pack(member, gate_input, groups), query_rows))

    t, kt, ktail, w, d, p, last, maps = key_terms(member, packed, edges, filter_key)
    maps = to_runners(maps)
    u, z, adds = value_terms(member, value_rows, edges, filter_value, t, ktail, d, last)
    adds, maps = after_all([adds, maps], [])
    adds = columns_to_runners(adds)
    f, g = query_terms(member, query_rows, edges, packed, filter_query, kt, w, p, u, z)
    adds, f, g = after_all([adds, f, g], [])
    state = from_runners(handoff(maps, adds), heads)

    gain = norm_gain.reshape(1, DV)
    swap = [(i, i ^ 1) for i in range(groups)]
    other_weight = lax.ppermute(out_weight, "head", swap)
    theirs = normed_rows(member, f, g, state, gate_rows[1::2], gain, 1)
    theirs = lax.ppermute(theirs, "head", swap)
    mine = normed_rows(member, f, g, state, gate_rows[0::2], gain, 0)
    width = out_weight.shape[1]
    cuts = 2
    totals = []
    for cut in range(cuts):
        kept, *sent = projected(
            mine, theirs, out_weight, other_weight, cut * width // cuts, width // cuts
        )
        totals.append(
            [kept]
            + [
                lax.ppermute(part, "head", [(i, i ^ (2 * step + 2)) for i in range(groups)])
                for step, part in enumerate(sent)
            ]
        )
    return jnp.concatenate(
        [sum(x.astype(f32) for x in parts).astype(bf16) for parts in totals], axis=1
    )


def solution(mesh):
    tokens = P(("seq", "head"), None)
    placed = (tokens,) * 6 + (P(None, "head"),) * 3 + (P(), P("head", None))
    return jax.shard_map(
        on_device, mesh=mesh, in_specs=placed, out_specs=tokens, check_vma=False
    )
```

```python
import functools

import jax
import jax.numpy as jnp
from jax import lax
from jax.experimental import pallas as pl
from jax.experimental.pallas import tpu as pltpu
from jax.sharding import PartitionSpec as P

HK = 16
HV = 32
DK = 128
DV = 128
CH = 128
EDGE = 16
SHARE = HV // HK
ODD_ROWS = 16

norm_floor = 1e-06
f32 = jnp.float32
bf16 = jnp.bfloat16


def params(megabytes=60):
    return pltpu.CompilerParams(vmem_limit_bytes=megabytes * 1024 * 1024)


def split(x):
    high = x.astype(bf16)
    return high, (x - high.astype(f32)).astype(bf16)


def as_left(x):
    return jnp.concatenate(split(x), axis=1)


def right_of(high, low):
    row = jnp.concatenate([high, low], axis=1)
    return jnp.concatenate([row, row], axis=0)


def as_right(x):
    return right_of(*split(x))


def product(left, right):
    both = jnp.dot(left, right, preferred_element_type=f32)
    half = both.shape[1] // 2
    return both[:, :half] + both[:, half:]


def grids():
    row = lax.broadcasted_iota(jnp.int32, (CH, CH), 0)
    column = lax.broadcasted_iota(jnp.int32, (CH, CH), 1)
    return row, column


def ones_where(mask):
    return jnp.where(mask, 1.0, 0.0).astype(bf16)


def place(me, pieces, out, margin):
    size = pieces[0].shape[0]
    for d, piece in enumerate(pieces):
        at = pl.multiple_of((me ^ d) * size + margin, 8)
        out[pl.ds(at, size), :] = piece[...].astype(out.dtype)


def place_gates(me, pieces, out, heads, size):
    for d, piece in enumerate(pieces):
        ends = piece[...].astype(f32)[12:16]
        sets = [ends[:, i * size : (i + 1) * size] for i in range(heads // 2)]
        rows = jnp.concatenate(sets + [jnp.zeros((128 - 2 * heads, size), f32)], axis=0)
        at = pl.multiple_of((me ^ d) * size, 16)
        out[pl.ds(at, size), :] = jnp.transpose(rows).astype(bf16)


def conv_silu(me, pieces, edge, taps_ref, padded):
    length = padded.shape[0] - 8
    taps = taps_ref[...].astype(f32)
    padded[8 - edge.shape[0] : 8] = edge
    place(me, pieces, padded, 8)
    margin = taps.shape[0] - 1
    summed = taps[margin : margin + 1] * padded[8 : 8 + length]
    for offset in range(margin):
        start = 8 - margin + offset
        summed = summed + taps[offset : offset + 1] * padded[start : start + length]
    return summed / (1.0 + jnp.exp(-summed))


def unit_rows(field):
    return field * lax.rsqrt(jnp.sum(field * field, axis=-1, keepdims=True) + norm_floor)


def strengths_and_rates(gates, first, count, heads):
    lane = lax.broadcasted_iota(jnp.int32, (gates.shape[1], CH), 0)
    picks = [ones_where(lane == first + e) for e in range(count)]
    picks += [ones_where(lane == heads + first + e) for e in range(count)]
    picked = jnp.dot(gates, jnp.concatenate(picks, axis=1), preferred_element_type=f32)
    return picked[:, : count * CH], picked[:, count * CH :].astype(bf16)


def decay_terms(rates, count):
    row, column = grids()
    below = ones_where(column <= row)
    pieces = []
    for e in range(count):
        rate = rates[:, e * CH : (e + 1) * CH]
        pieces += [jnp.where(row > column, rate, jnp.zeros_like(rate)), rate]
    sums = jnp.dot(below, jnp.concatenate(pieces, axis=1), preferred_element_type=f32)
    ratios, growth = [], []
    for e in range(count):
        at = 2 * e * CH
        ratios.append(jnp.where(column <= row, jnp.exp(sums[:, at : at + CH]), 0.0))
        growth.append(jnp.exp(sums[:, at + CH : at + 2 * CH]))
    return ratios, growth


def unit_lower_inverses(lower):
    row, column = grids()
    names = list(lower)
    eye = jnp.where(row == column, 1.0, 0.0)
    pair = (row // 2 == column // 2) & (column < row)
    halves = {n: split(lower[n]) for n in names}
    inverse = {n: eye - jnp.where(pair, lower[n], 0.0) for n in names}
    size = 2
    while size < CH:
        mask = ones_where(
            (row // (2 * size) == column // (2 * size))
            & ((row // size) % 2 == 1)
            & ((column // size) % 2 == 0)
        )
        rounded = {n: inverse[n].astype(bf16) for n in names}
        if size < ODD_ROWS:
            first = {
                n: jnp.dot(halves[n][0] * mask, rounded[n], preferred_element_type=f32).astype(bf16)
                for n in names
            }
            for n in names:
                inverse[n] = inverse[n] - jnp.dot(rounded[n], first[n], preferred_element_type=f32)
        else:
            starts = range(size, CH, 2 * size)

            def odd(x):
                return jnp.concatenate([x[s : s + size] for s in starts], axis=0)

            def back(x, even):
                rows = []
                for i, s in enumerate(starts):
                    rows += [even[s - size : s], x[i * size : (i + 1) * size]]
                return jnp.concatenate(rows, axis=0)

            some = odd(mask)
            nothing = jnp.zeros((CH, CH), bf16)
            first = {
                n: jnp.dot(
                    odd(halves[n][0]) * some, rounded[n], preferred_element_type=f32
                ).astype(bf16)
                for n in names
            }
            for n in names:
                change = jnp.dot(
                    odd(rounded[n]), back(first[n], nothing), preferred_element_type=f32
                )
                inverse[n] = back(odd(inverse[n]) - change, inverse[n])
        size *= 2
    parts = {n: split(inverse[n]) for n in names}
    left = {
        n: (
            eye
            - inverse[n]
            - product(jnp.concatenate(halves[n], axis=1), right_of(*parts[n]))
        ).astype(bf16)
        for n in names
    }
    return {
        n: inverse[n] + jnp.dot(parts[n][0], left[n], preferred_element_type=f32) for n in names
    }


def key_kernel(groups_count, heads, member, *refs):
    pieces, refs = refs[:groups_count], refs[groups_count:]
    gate_pieces, refs = refs[:groups_count], refs[groups_count:]
    edge, taps, t_out, kt_out, ktail_out, w_out, d_out, p_out, last_out, map_out, padded, gates = refs
    here = pieces[0].shape[1] // DK
    count = here * SHARE
    blocks = gates.shape[0] // CH
    me = member[0]
    first = pl.program_id(0) * count
    filtered = conv_silu(me, pieces, edge[...].astype(f32)[EDGE - 8 :], taps, padded)
    place_gates(me, gate_pieces, gates, heads, pieces[0].shape[0])
    row, column = grids()
    eye = jnp.where(row == column, 1.0, 0.0)
    groups = [(c, k) for c in range(blocks) for k in range(here)]
    problems = [(c, e) for c in range(blocks) for e in range(count)]

    def chunk_of(x, c):
        return x[c * CH : (c + 1) * CH]

    strengths, rates = strengths_and_rates(gates[...], first, count, heads)
    unit = [unit_rows(filtered[:, k * DK : (k + 1) * DK]) for k in range(here)]
    decays = [decay_terms(chunk_of(rates, c), count) for c in range(blocks)]
    keys = {(c, k): chunk_of(unit[k], c) for c, k in groups}
    turned = {g: jnp.transpose(keys[g]) for g in groups}
    sides = {g: split(turned[g]) for g in groups}
    kk = {g: product(as_left(keys[g]), right_of(*sides[g])) for g in groups}
    lane = lax.broadcasted_iota(jnp.int32, (8, gates.shape[1]), 1)
    order = lax.broadcasted_iota(jnp.int32, (8, gates.shape[1]), 0)
    pick = ones_where(lane == first + order)
    across = [
        lax.dot_general(
            pick,
            gates[c * CH : (c + 1) * CH, :],
            (((1,), (1,)), ((), ())),
            preferred_element_type=f32,
        )
        for c in range(blocks)
    ]
    lower, ktail = {}, {}
    for c, k in groups:
        kt_out[k, c] = jnp.concatenate(sides[c, k], axis=1)
    for c, e in problems:
        ratios, growth = decays[c][0][e], decays[c][1][e]
        strength = chunk_of(strengths, c)[:, e * CH : (e + 1) * CH]
        k = e // SHARE
        lower[c, e] = jnp.where(column < row, strength * kk[c, k] * ratios, 0.0)
        ktail[c, e] = as_left(turned[c, k] * ratios[CH - 1 : CH])
        ktail_out[k, c, e % SHARE] = ktail[c, e]
        last_out[k, c, e % SHARE] = growth[CH - 8 : CH]
    inverse = unit_lower_inverses(lower)
    solving = {(c, e): as_left(inverse[c, e] * across[c][e : e + 1]) for c, e in problems}
    solved = {
        (c, e): product(solving[c, e], as_right(decays[c][1][e] * keys[c, e // SHARE]))
        for c, e in problems
    }
    erasing = {pc: split(solved[pc]) for pc in problems}
    maps = {pc: as_left(product(ktail[pc], right_of(*erasing[pc]))) for pc in problems}
    for c, e in problems:
        k = e // SHARE
        t_out[k, c, e % SHARE] = solving[c, e]
        w_out[k, c, e % SHARE] = jnp.concatenate(erasing[c, e], axis=1)
        d_out[k, c, e % SHARE] = maps[c, e]
    running = []
    for e in range(count):
        high, low = maps[0, e][:, :DK], maps[0, e][:, DK:]
        running.append(
            decays[0][1][e][CH - 1 : CH] * eye - (high.astype(f32) + low.astype(f32))
        )
    for c in range(1, blocks):
        parts = [split(x) for x in running]
        for e in range(count):
            p_out[e // SHARE, c - 1, e % SHARE] = jnp.concatenate(parts[e], axis=1)
        running = [
            decays[c][1][e][CH - 1 : CH] * running[e] - product(maps[c, e], right_of(*parts[e]))
            for e in range(count)
        ]
    for e in range(count):
        map_out[e] = (eye - running[e]).astype(bf16)


def right_from(both):
    return jnp.concatenate([both, both], axis=0)


def value_kernel(groups_count, member, *refs):
    pieces, refs = refs[:groups_count], refs[groups_count:]
    edge, taps, t_in, ktail, d_in, last, maps, u_out, z_out, span_out, padded, before = refs
    blocks = t_in.shape[1]
    width = pieces[0].shape[1]
    count = width // DV
    ends = edge[...].astype(f32)
    for r in range(SHARE):
        before[:, r * edge.shape[1] : (r + 1) * edge.shape[1]] = ends[4 * r : 4 * r + 4]
    at = pl.multiple_of(pl.program_id(0) * width, 128)
    values = conv_silu(member[0], pieces, before[:, pl.ds(at, width)], taps, padded)
    problems = [(c, e) for c in range(blocks) for e in range(count)]

    def at(ref, c, e):
        return ref[e // SHARE, c, e % SHARE]

    written = {
        (c, e): split(
            product(
                at(t_in, c, e),
                as_right(values[c * CH : (c + 1) * CH, e * DV : (e + 1) * DV]),
            )
        )
        for c, e in problems
    }
    adds = {pc: product(at(ktail, *pc), right_of(*written[pc])) for pc in problems}
    for c, e in problems:
        u_out[e // SHARE, c, e % SHARE] = jnp.concatenate(written[c, e], axis=1)
    running = [adds[0, e] for e in range(count)]
    for c in range(1, blocks):
        parts = [split(x) for x in running]
        for e in range(count):
            z_out[e // SHARE, c - 1, e % SHARE] = jnp.concatenate(parts[e], axis=1)
        running = [
            at(last, c, e)[7:8] * running[e]
            - product(at(d_in, c, e), right_of(*parts[e]))
            + adds[c, e]
            for e in range(count)
        ]
    for e in range(count):
        span_out[e, :, :DK] = maps[e]
        span_out[e, :, DK:] = running[e].astype(bf16)


def query_kernel(groups_count, heads, member, *refs):
    pieces, refs = refs[:groups_count], refs[groups_count:]
    gate_pieces, refs = refs[:groups_count], refs[groups_count:]
    edge, taps, kt_in, w_in, p_in, u_in, z_in, f_out, g_out, padded, gates = refs
    here = pieces[0].shape[1] // DK
    count = here * SHARE
    blocks = gates.shape[0] // CH
    me = member[0]
    first = pl.program_id(0) * count
    filtered = conv_silu(me, pieces, edge[...].astype(f32)[8:12], taps, padded)
    place_gates(me, gate_pieces, gates, heads, pieces[0].shape[0])
    unit = [unit_rows(filtered[:, k * DK : (k + 1) * DK]) * DK ** (-0.5) for k in range(here)]
    problems = [(c, e) for c in range(blocks) for e in range(count)]
    strengths, rates = strengths_and_rates(gates[...], first, count, heads)
    decays = [decay_terms(rates[c * CH : (c + 1) * CH], count) for c in range(blocks)]

    def at(ref, c, e):
        return right_from(ref[e // SHARE, c, e % SHARE])

    queries = {
        (c, k): unit[k][c * CH : (c + 1) * CH] for c in range(blocks) for k in range(here)
    }
    qk = {
        (c, k): product(as_left(queries[c, k]), right_from(kt_in[k, c])) for c, k in queries
    }
    mix = {(c, e): as_left(qk[c, e // SHARE] * decays[c][0][e]) for c, e in problems}
    entry = {
        (c, e): as_left(
            decays[c][1][e] * queries[c, e // SHARE] - product(mix[c, e], at(w_in, c, e))
        )
        for c, e in problems
    }
    local = {pc: product(mix[pc], at(u_in, *pc)) for pc in problems}
    for c, e in problems:
        here = slice(c * CH, (c + 1) * CH)
        if c == 0:
            f_out[e, here] = entry[c, e][:, :DK]
            g_out[e, here] = local[c, e].astype(bf16)
        else:
            f_out[e, here] = product(entry[c, e], at(p_in, c - 1, e)).astype(bf16)
            total = local[c, e] + product(entry[c, e], at(z_in, c - 1, e))
            g_out[e, here] = total.astype(bf16)


def handoff_kernel(spans_in, out):
    spans, heads, width = out.shape[0], out.shape[1], out.shape[3]
    running = [jnp.zeros(out.shape[2:], f32) for h in range(heads)]
    for j in range(spans):
        for h in range(heads):
            out[j, h] = running[h].astype(bf16)
        if j + 1 < spans:
            for h in range(heads):
                erased = jnp.dot(
                    spans_in[j, h, :, :DK],
                    jnp.concatenate(split(running[h]), axis=1),
                    preferred_element_type=f32,
                )
                erased = erased[:, :width] + erased[:, width:]
                running[h] = running[h] - erased + spans_in[j, h, :, DK:].astype(f32)


def norm_kernel(count, member, *refs):
    f_in, refs = refs[:count], refs[count:]
    g_in, refs = refs[:count], refs[count:]
    gate, refs = refs[:count], refs[count:]
    state, gain, out = refs
    cells = [(i, h) for i in range(count) for h in range(state.shape[0])]
    core = {
        (i, h): g_in[i][h].astype(f32)
        + jnp.dot(f_in[i][h], state[h], preferred_element_type=f32)
        for i, h in cells
    }
    scale = {
        n: lax.rsqrt(jnp.mean(core[n] * core[n], axis=-1, keepdims=True) + norm_floor)
        for n in cells
    }
    for i, h in cells:
        columns = slice(h * DV, (h + 1) * DV)
        gates = gate[i][:, columns].astype(f32)
        gates = gates / (1.0 + jnp.exp(-gates))
        out[i, :, columns] = (core[i, h] * scale[i, h] * gain[...] * gates).astype(bf16)


def project_kernel(mine, theirs, own_weight, other_weight, kept, *sent):
    rows, depth = mine.shape[0] * mine.shape[1], mine.shape[2]
    product_ = jnp.dot(
        mine[...].reshape(rows, depth), own_weight[...], preferred_element_type=f32
    ) + jnp.dot(theirs[...].reshape(rows, depth), other_weight[...], preferred_element_type=f32)
    size = mine.shape[1]
    kept[...] = product_[:size]
    for i, out in enumerate(sent):
        out[...] = product_[(i + 1) * size : (i + 2) * size].astype(bf16)


def pack_kernel(groups_count, member, *refs):
    array, outs = refs[0], refs[1:]
    me = member[0]
    width = array.shape[1] // groups_count
    for d in range(groups_count):
        at = pl.multiple_of((me ^ d) * width, 128)
        outs[d][...] = array[:, pl.ds(at, width)]


def pack_keys_kernel(groups_count, member, *refs):
    key, value_end, query_end, strength, decay = refs[:5]
    outs = refs[5:]
    me = member[0]
    tokens, width = key.shape[0], key.shape[1] // groups_count
    heads = HV // groups_count
    gates = jnp.concatenate([strength[...], decay[...]], axis=0)
    row = lax.broadcasted_iota(jnp.int32, (2 * heads, 2 * HV), 0)
    column = lax.broadcasted_iota(jnp.int32, (2 * heads, 2 * HV), 1)
    for d in range(groups_count):
        at = me ^ d
        outs[d][:tokens] = key[:, pl.ds(pl.multiple_of(at * width, 128), width)]
        ends = []
        for r in range(SHARE):
            start = pl.multiple_of((at * SHARE + r) * width, 128)
            ends.append(value_end[:, pl.ds(start, width)].astype(f32)[EDGE - 4 :])
        start = pl.multiple_of(at * width, 128)
        ends.append(query_end[:, pl.ds(start, width)].astype(f32)[EDGE - 4 :])
        wanted = jnp.where(row < heads, row, row - heads + HV) + at * heads
        picked = jnp.dot(ones_where(column == wanted), gates, preferred_element_type=f32)
        sets = [picked[4 * i : 4 * i + 4] for i in range(heads // 2)]
        if width > tokens * len(sets):
            sets.append(jnp.zeros((4, width - tokens * len(sets)), f32))
        ends.append(jnp.concatenate(sets, axis=1))
        outs[d][tokens:] = jnp.concatenate(ends, axis=0).astype(bf16)


def shape(dims, kind):
    return jax.ShapeDtypeStruct(dims, kind)


def pack(member, array, groups):
    tokens, width = array.shape[0], array.shape[1] // groups
    return pl.pallas_call(
        functools.partial(pack_kernel, groups),
        grid_spec=grid_of(
            1,
            [pl.BlockSpec(array.shape, lambda p, me: (0, 0))],
            [pl.BlockSpec((tokens, width), lambda p, me: (0, 0))] * groups,
            [],
        ),
        out_shape=[shape((tokens, width), bf16)] * groups,
        compiler_params=params(),
        cost_estimate=cost(3),
        name="pack",
    )(member, array)


def pack_keys(member, key, value, query, strength, decay, groups):
    tokens, width = key.shape[0], key.shape[1] // groups

    def whole(dims):
        return pl.BlockSpec(dims, lambda p, me: (0, 0))

    def end(x):
        return pl.BlockSpec((EDGE, x.shape[1]), lambda p, me: (tokens // EDGE - 1, 0))

    packed = (tokens + EDGE, width)
    return pl.pallas_call(
        functools.partial(pack_keys_kernel, groups),
        grid_spec=grid_of(
            1,
            [whole(key.shape), end(value), end(query), whole(strength.shape), whole(decay.shape)],
            [whole(packed)] * groups,
            [],
        ),
        out_shape=[shape(packed, bf16)] * groups,
        compiler_params=params(),
        cost_estimate=cost(3),
        name="pack_keys",
    )(member, key, value, query, strength, decay)


def per_head(each, dims):
    return pl.BlockSpec((each,) + dims, lambda p, me: (p,) + (0,) * len(dims))


def columns_of(rows, width):
    return pl.BlockSpec((rows, width), lambda p, me: (0, p))


def heads_at_once(key_heads):
    return 2 if key_heads % 2 == 0 else 1


def cost(microseconds):
    return pl.CostEstimate(
        flops=int(microseconds * 1e9), bytes_accessed=int(microseconds * 3e6), transcendentals=0
    )


def grid_of(steps, in_specs, out_specs, scratch):
    return pltpu.PrefetchScalarGridSpec(
        num_scalar_prefetch=1,
        grid=(steps,),
        in_specs=in_specs,
        out_specs=out_specs,
        scratch_shapes=scratch,
    )


def key_terms(member, packed, edge, taps):
    groups = len(packed)
    own = packed[0].shape[0] - EDGE
    tokens = groups * own
    key_heads = taps.shape[1] // DK
    each = heads_at_once(key_heads)
    blocks = tokens // CH
    wide = (blocks, SHARE, CH, 2 * CH)
    kinds = [
        wide,
        (blocks, DK, 2 * CH),
        wide,
        wide,
        wide,
        (blocks - 1, SHARE, DK, 2 * DK),
        (blocks, SHARE, 8, CH),
    ]
    types = [bf16] * 6 + [f32]
    return pl.pallas_call(
        functools.partial(key_kernel, groups, key_heads * SHARE),
        grid_spec=grid_of(
            key_heads // each,
            [columns_of(own, each * DK)] * groups
            + [pl.BlockSpec((EDGE, key_heads * DK), lambda p, me: (own // EDGE, 0))] * groups
            + [columns_of(EDGE, each * DK)]
            + [columns_of(taps.shape[0], each * DK)],
            [per_head(each, kind) for kind in kinds]
            + [pl.BlockSpec((each * SHARE, DK, DK), lambda p, me: (p, 0, 0))],
            [pltpu.VMEM((tokens + 8, each * DK), f32), pltpu.VMEM((tokens, 128), bf16)],
        ),
        out_shape=[shape((key_heads,) + kind, t) for kind, t in zip(kinds, types)]
        + [shape((key_heads * SHARE, DK, DK), bf16)],
        compiler_params=params(),
        cost_estimate=cost(12),
        name="key_terms",
    )(member, *packed, *packed, edge, taps)


def value_terms(member, pieces, edge, taps, t_in, ktail, d_in, last, maps):
    groups = len(pieces)
    own = pieces[0].shape[0]
    tokens = groups * own
    key_heads = t_in.shape[0]
    each = heads_at_once(key_heads)
    blocks = tokens // CH
    width = each * SHARE * DV
    return pl.pallas_call(
        functools.partial(value_kernel, groups),
        grid_spec=grid_of(
            key_heads // each,
            [columns_of(own, width)] * groups
            + [pl.BlockSpec((EDGE, key_heads * DK), lambda p, me: (1, 0))]
            + [columns_of(taps.shape[0], width)]
            + [per_head(each, x.shape[1:]) for x in (t_in, ktail, d_in, last)]
            + [pl.BlockSpec((each * SHARE, DK, DK), lambda p, me: (p, 0, 0))],
            [
                per_head(each, (blocks, SHARE, CH, 2 * DV)),
                per_head(each, (blocks - 1, SHARE, DK, 2 * DV)),
                pl.BlockSpec((each * SHARE, DK, DK + DV), lambda p, me: (p, 0, 0)),
            ],
            [
                pltpu.VMEM((tokens + 8, width), f32),
                pltpu.VMEM((4, key_heads * SHARE * DV), f32),
            ],
        ),
        out_shape=[
            shape((key_heads, blocks, SHARE, CH, 2 * DV), bf16),
            shape((key_heads, blocks - 1, SHARE, DK, 2 * DV), bf16),
            shape((key_heads * SHARE, DK, DK + DV), bf16),
        ],
        compiler_params=params(),
        cost_estimate=cost(7),
        name="value_terms",
    )(member, *pieces, edge, taps, t_in, ktail, d_in, last, maps)


def query_terms(member, pieces, edge, packed, taps, kt, w, p, u, z):
    groups = len(pieces)
    own = pieces[0].shape[0]
    tokens = groups * own
    key_heads = kt.shape[0]
    each = heads_at_once(key_heads)
    out = pl.BlockSpec((each * SHARE, tokens, DK), lambda p, me: (p, 0, 0))
    return pl.pallas_call(
        functools.partial(query_kernel, groups, key_heads * SHARE),
        grid_spec=grid_of(
            key_heads // each,
            [columns_of(own, each * DK)] * groups
            + [pl.BlockSpec((EDGE, key_heads * DK), lambda p, me: (own // EDGE, 0))] * groups
            + [pl.BlockSpec((EDGE, each * DK), lambda p, me: (1, p))]
            + [columns_of(taps.shape[0], each * DK)]
            + [per_head(each, x.shape[1:]) for x in (kt, w, p, u, z)],
            [out, out],
            [pltpu.VMEM((tokens + 8, each * DK), f32), pltpu.VMEM((tokens, 128), bf16)],
        ),
        out_shape=[shape((key_heads * SHARE, tokens, DK), bf16)] * 2,
        compiler_params=params(),
        cost_estimate=cost(9),
        name="query_terms",
    )(member, *pieces, *packed, edge, taps, kt, w, p, u, z)


def handoff(spans):
    dims = spans.shape[:3] + (spans.shape[3] - DK,)
    return pl.pallas_call(
        handoff_kernel,
        out_shape=shape(dims, bf16),
        compiler_params=params(16),
        cost_estimate=cost(1),
        name="handoff",
    )(spans)


def normed_rows(member, f, g, state, gate, gain, parity):
    heads = state.shape[0]
    count = len(gate)
    size, width = gate[0].shape

    def token_block(i):
        return pl.BlockSpec(
            (heads, size, DK), lambda p, me: (0, me[0] ^ (2 * i + parity), 0)
        )

    whole = pl.BlockSpec((size, width), lambda p, me: (0, 0))
    return pl.pallas_call(
        functools.partial(norm_kernel, count),
        grid_spec=grid_of(
            1,
            [token_block(i) for i in range(count)] * 2
            + [whole] * count
            + [
                pl.BlockSpec((heads, DK, DV), lambda p, me: (0, 0, 0)),
                pl.BlockSpec((1, DV), lambda p, me: (0, 0)),
            ],
            pl.BlockSpec((count, size, width), lambda p, me: (0, 0, 0)),
            [],
        ),
        out_shape=shape((count, size, width), bf16),
        compiler_params=params(16),
        cost_estimate=cost(1),
        name="normed_rows",
    )(member, *([f] * count), *([g] * count), *gate, state, gain)


def projected(mine, theirs, own_weight, other_weight, start, width):
    ranks, size, depth = mine.shape
    tile = min(width, 512)
    whole = pl.BlockSpec((ranks, size, depth), lambda j: (0, 0, 0))
    weight = pl.BlockSpec((depth, tile), lambda j: (0, j + start // tile))
    out = pl.BlockSpec((size, tile), lambda j: (0, j))
    return pl.pallas_call(
        project_kernel,
        grid=(width // tile,),
        in_specs=[whole, whole, weight, weight],
        out_specs=[out] * ranks,
        out_shape=[shape((size, width), f32)] + [shape((size, width), bf16)] * (ranks - 1),
        compiler_params=params(16),
        cost_estimate=cost(3),
        name="projected",
    )(mine, theirs, own_weight, other_weight)


def sum_kernel(cuts, *refs):
    parts, out = refs[:-1], refs[-1]
    each = len(parts) // cuts
    for cut in range(cuts):
        total = parts[cut * each][...]
        for part in parts[cut * each + 1 : (cut + 1) * each]:
            total = total + part[...].astype(f32)
        width = total.shape[1]
        out[:, cut * width : (cut + 1) * width] = total.astype(bf16)


def summed_parts(parts, cuts):
    rows, width = parts[0].shape
    return pl.pallas_call(
        functools.partial(sum_kernel, cuts),
        out_shape=shape((rows, width * cuts), bf16),
        compiler_params=params(16),
        cost_estimate=cost(1),
        name="summed_parts",
    )(*parts)


def to_members(pieces):
    groups = len(pieces)
    return [pieces[0]] + [
        lax.ppermute(pieces[d], "head", [(i, i ^ d) for i in range(groups)])
        for d in range(1, groups)
    ]


def after_all(values, others):
    return lax.optimization_barrier((*values, *others))[: len(values)]


def to_runners(terms):
    spans = lax.axis_size("seq")
    heads = terms.shape[0]
    if spans <= heads:
        pieces = terms.reshape(spans, heads // spans, DK, DK + DV)
    else:
        cuts = spans // heads
        maps = jnp.repeat(terms[:, :, :DK], cuts, axis=0)
        adds = terms[:, :, DK:].reshape(heads, DK, cuts, DV // cuts)
        adds = adds.transpose(0, 2, 1, 3).reshape(spans, DK, DV // cuts)
        pieces = jnp.concatenate([maps, adds], axis=2)[:, None]
    return lax.all_to_all(pieces, "seq", 0, 0)


def from_runners(entries, heads):
    spans, each, depth, width = entries.shape
    entries = lax.all_to_all(entries, "seq", 0, 0)
    entries = entries.reshape(heads // each, DV // width, each, depth, width)
    return entries.transpose(0, 2, 3, 1, 4).reshape(heads, depth, DV)


def on_device(
    query_input,
    key_input,
    value_input,
    gate_input,
    write_strength,
    log_decay,
    filter_query,
    filter_key,
    filter_value,
    norm_gain,
    out_weight,
):
    groups = lax.axis_size("head")
    spans = lax.axis_size("seq")
    member = lax.axis_index("head").astype(jnp.int32).reshape(1)
    heads = filter_value.shape[1] // DV

    key_out = pack_keys(
        member, key_input, value_input, query_input, write_strength.T, log_decay.T, groups
    )
    packed = to_members(key_out)
    edge = packed[0][-2 * EDGE :]
    for d in range(1, groups):
        edge = jnp.where((member[0] ^ d) == groups - 1, packed[d][-2 * EDGE :], edge)
    value_out = pack(member, value_input, groups)
    query_out = pack(member, query_input, groups)
    gate_out = pack(member, gate_input, groups)
    edge, *value_out = after_all([edge, *value_out], [*query_out, *gate_out])
    edge = lax.ppermute(edge, "seq", [(s, s + 1) for s in range(spans - 1)])
    value_rows = to_members(value_out)
    t, kt, ktail, w, d, p, last, maps = key_terms(member, packed, edge, filter_key)
    u, z, terms = value_terms(
        member, value_rows, edge, filter_value, t, ktail, d, last, maps
    )
    query_rows = to_members(after_all(query_out, [terms]))
    gate_rows = to_members(after_all(gate_out, [terms]))
    (own_weight,) = after_all([out_weight], [terms])
    swap = [(i, i ^ 1) for i in range(groups)]
    other_weight = lax.ppermute(own_weight, "head", swap)
    terms = to_runners(terms)
    entries = handoff(terms)
    query_rows = after_all(query_rows, [entries, *gate_rows])
    f, g = query_terms(member, query_rows, edge, packed, filter_query, kt, w, p, u, z)
    state = from_runners(entries, heads)

    gain = norm_gain.reshape(1, DV)
    theirs = normed_rows(member, f, g, state, gate_rows[1::2], gain, 1)
    theirs = lax.ppermute(theirs, "head", swap)
    mine = normed_rows(member, f, g, state, gate_rows[0::2], gain, 0)
    width = out_weight.shape[1]
    cuts = 2
    parts = []
    for cut in range(cuts):
        kept, *sent = projected(
            mine, theirs, out_weight, other_weight, cut * width // cuts, width // cuts
        )
        parts.append(kept)
        parts += [
            lax.ppermute(part, "head", [(i, i ^ (2 * step + 2)) for i in range(groups)])
            for step, part in enumerate(sent)
        ]
    return summed_parts(parts, cuts)


def solution(mesh):
    tokens = P(("seq", "head"), None)
    placed = (tokens,) * 6 + (P(None, "head"),) * 3 + (P(), P("head", None))
    return jax.shard_map(
        on_device, mesh=mesh, in_specs=placed, out_specs=tokens, check_vma=False
    )
```

```python
import functools

import jax
import jax.numpy as jnp
from jax import lax
from jax.experimental import pallas as pl
from jax.experimental.pallas import tpu as pltpu
from jax.sharding import PartitionSpec as P

HK = 16
HV = 32
DK = 128
DV = 128
CH = 128
EDGE = 16
SHARE = HV // HK
ODD_ROWS = 16

norm_floor = 1e-06
f32 = jnp.float32
bf16 = jnp.bfloat16


def params(megabytes=60):
    return pltpu.CompilerParams(vmem_limit_bytes=megabytes * 1024 * 1024)


def split(x):
    high = x.astype(bf16)
    return high, (x - high.astype(f32)).astype(bf16)


def as_left(x):
    return jnp.concatenate(split(x), axis=1)


def right_of(high, low):
    row = jnp.concatenate([high, low], axis=1)
    return jnp.concatenate([row, row], axis=0)


def as_right(x):
    return right_of(*split(x))


def product(left, right):
    both = jnp.dot(left, right, preferred_element_type=f32)
    half = both.shape[1] // 2
    return both[:, :half] + both[:, half:]


def grids():
    row = lax.broadcasted_iota(jnp.int32, (CH, CH), 0)
    column = lax.broadcasted_iota(jnp.int32, (CH, CH), 1)
    return row, column


def ones_where(mask):
    return jnp.where(mask, 1.0, 0.0).astype(bf16)


def place(me, pieces, out, margin):
    size = pieces[0].shape[0]
    for d, piece in enumerate(pieces):
        at = pl.multiple_of((me ^ d) * size + margin, 8)
        out[pl.ds(at, size), :] = piece[...].astype(out.dtype)


def place_gates(me, pieces, out, heads, size):
    for d, piece in enumerate(pieces):
        ends = piece[...].astype(f32)[12:16]
        sets = [ends[:, i * size : (i + 1) * size] for i in range(heads // 2)]
        rows = jnp.concatenate(sets + [jnp.zeros((128 - 2 * heads, size), f32)], axis=0)
        at = pl.multiple_of((me ^ d) * size, 16)
        out[pl.ds(at, size), :] = jnp.transpose(rows).astype(bf16)


def conv_silu(me, pieces, edge, taps_ref, padded):
    length = padded.shape[0] - 8
    taps = taps_ref[...].astype(f32)
    padded[8 - edge.shape[0] : 8] = edge
    place(me, pieces, padded, 8)
    margin = taps.shape[0] - 1
    summed = taps[margin : margin + 1] * padded[8 : 8 + length]
    for offset in range(margin):
        start = 8 - margin + offset
        summed = summed + taps[offset : offset + 1] * padded[start : start + length]
    return summed / (1.0 + jnp.exp(-summed))


def unit_rows(field):
    return field * lax.rsqrt(jnp.sum(field * field, axis=-1, keepdims=True) + norm_floor)


def strengths_and_rates(gates, first, count, heads):
    lane = lax.broadcasted_iota(jnp.int32, (gates.shape[1], CH), 0)
    picks = [ones_where(lane == first + e) for e in range(count)]
    picks += [ones_where(lane == heads + first + e) for e in range(count)]
    picked = jnp.dot(gates, jnp.concatenate(picks, axis=1), preferred_element_type=f32)
    return picked[:, : count * CH], picked[:, count * CH :].astype(bf16)


def decay_terms(rates, count):
    row, column = grids()
    below = ones_where(column <= row)
    pieces = []
    for e in range(count):
        rate = rates[:, e * CH : (e + 1) * CH]
        pieces += [jnp.where(row > column, rate, jnp.zeros_like(rate)), rate]
    sums = jnp.dot(below, jnp.concatenate(pieces, axis=1), preferred_element_type=f32)
    ratios, growth = [], []
    for e in range(count):
        at = 2 * e * CH
        ratios.append(jnp.where(column <= row, jnp.exp(sums[:, at : at + CH]), 0.0))
        growth.append(jnp.exp(sums[:, at + CH : at + 2 * CH]))
    return ratios, growth


def unit_lower_inverses(lower):
    row, column = grids()
    names = list(lower)
    eye = jnp.where(row == column, 1.0, 0.0)
    pair = (row // 2 == column // 2) & (column < row)
    halves = {n: split(lower[n]) for n in names}
    inverse = {n: eye - jnp.where(pair, lower[n], 0.0) for n in names}
    size = 2
    while size < CH:
        mask = ones_where(
            (row // (2 * size) == column // (2 * size))
            & ((row // size) % 2 == 1)
            & ((column // size) % 2 == 0)
        )
        rounded = {n: inverse[n].astype(bf16) for n in names}
        if size < ODD_ROWS:
            first = {
                n: jnp.dot(halves[n][0] * mask, rounded[n], preferred_element_type=f32).astype(bf16)
                for n in names
            }
            for n in names:
                inverse[n] = inverse[n] - jnp.dot(rounded[n], first[n], preferred_element_type=f32)
        else:
            starts = range(size, CH, 2 * size)

            def odd(x):
                return jnp.concatenate([x[s : s + size] for s in starts], axis=0)

            def back(x, even):
                rows = []
                for i, s in enumerate(starts):
                    rows += [even[s - size : s], x[i * size : (i + 1) * size]]
                return jnp.concatenate(rows, axis=0)

            some = odd(mask)
            nothing = jnp.zeros((CH, CH), bf16)
            first = {
                n: jnp.dot(
                    odd(halves[n][0]) * some, rounded[n], preferred_element_type=f32
                ).astype(bf16)
                for n in names
            }
            for n in names:
                change = jnp.dot(
                    odd(rounded[n]), back(first[n], nothing), preferred_element_type=f32
                )
                inverse[n] = back(odd(inverse[n]) - change, inverse[n])
        size *= 2
    parts = {n: split(inverse[n]) for n in names}
    left = {
        n: (
            eye
            - inverse[n]
            - product(jnp.concatenate(halves[n], axis=1), right_of(*parts[n]))
        ).astype(bf16)
        for n in names
    }
    return {
        n: inverse[n] + jnp.dot(parts[n][0], left[n], preferred_element_type=f32) for n in names
    }


def key_kernel(groups_count, heads, member, *refs):
    pieces, refs = refs[:groups_count], refs[groups_count:]
    gate_pieces, refs = refs[:groups_count], refs[groups_count:]
    edge, taps, t_out, kt_out, d_out, rows_out, map_out, padded, gates = refs
    here = pieces[0].shape[1] // DK
    count = here * SHARE
    blocks = gates.shape[0] // CH
    me = member[0]
    first = pl.program_id(0) * count
    filtered = conv_silu(me, pieces, edge[...].astype(f32)[EDGE - 8 :], taps, padded)
    place_gates(me, gate_pieces, gates, heads, pieces[0].shape[0])
    row, column = grids()
    eye = jnp.where(row == column, 1.0, 0.0)
    groups = [(c, k) for c in range(blocks) for k in range(here)]
    problems = [(c, e) for c in range(blocks) for e in range(count)]

    def chunk_of(x, c):
        return x[c * CH : (c + 1) * CH]

    strengths, rates = strengths_and_rates(gates[...], first, count, heads)
    unit = [unit_rows(filtered[:, k * DK : (k + 1) * DK]) for k in range(here)]
    decays = [decay_terms(chunk_of(rates, c), count) for c in range(blocks)]
    keys = {(c, k): chunk_of(unit[k], c) for c, k in groups}
    turned = {g: jnp.transpose(keys[g]) for g in groups}
    sides = {g: split(turned[g]) for g in groups}
    kk = {g: product(as_left(keys[g]), right_of(*sides[g])) for g in groups}
    lane = lax.broadcasted_iota(jnp.int32, (2 * count, gates.shape[1]), 1)
    order = lax.broadcasted_iota(jnp.int32, (2 * count, gates.shape[1]), 0)
    pick = ones_where(lane == first + jnp.where(order < count, order, order - count + heads))
    across = [
        lax.dot_general(
            pick,
            gates[c * CH : (c + 1) * CH, :],
            (((1,), (1,)), ((), ())),
            preferred_element_type=f32,
        )
        for c in range(blocks)
    ]
    growing = [
        jnp.exp(
            jnp.dot(across[c].astype(bf16), ones_where(row <= column), preferred_element_type=f32)
        )
        for c in range(blocks)
    ]
    lower, ktail = {}, {}
    for c, k in groups:
        kt_out[k, c] = jnp.concatenate(sides[c, k], axis=1)
    for c, e in problems:
        ratios, growth = decays[c][0][e], decays[c][1][e]
        strength = chunk_of(strengths, c)[:, e * CH : (e + 1) * CH]
        k = e // SHARE
        lower[c, e] = jnp.where(column < row, strength * kk[c, k] * ratios, 0.0)
        ktail[c, e] = (turned[c, k] * ratios[CH - 1 : CH]).astype(bf16)
        rows_out[k, c, e % SHARE] = jnp.concatenate(
            [ratios[CH - 1 : CH], growing[c][count + e : count + e + 1], growth[CH - 6 : CH]],
            axis=0,
        )
    inverse = unit_lower_inverses(lower)
    solving = {(c, e): as_left(inverse[c, e] * across[c][e : e + 1]) for c, e in problems}
    solved = {
        (c, e): jnp.dot(
            solving[c, e][:, :CH],
            (decays[c][1][e] * keys[c, e // SHARE]).astype(bf16),
            preferred_element_type=f32,
        ).astype(bf16)
        for c, e in problems
    }
    maps = {
        pc: jnp.dot(ktail[pc], solved[pc], preferred_element_type=f32).astype(bf16)
        for pc in problems
    }
    for c, e in problems:
        k = e // SHARE
        t_out[k, c, e % SHARE] = solving[c, e][:, :CH]
        d_out[k, c, e % SHARE] = maps[c, e]
    running = [
        decays[0][1][e][CH - 1 : CH] * eye - maps[0, e].astype(f32) for e in range(count)
    ]
    for c in range(1, blocks):
        running = [
            decays[c][1][e][CH - 1 : CH] * running[e]
            - jnp.dot(maps[c, e], running[e].astype(bf16), preferred_element_type=f32)
            for e in range(count)
        ]
    for e in range(count):
        map_out[e] = (eye - running[e]).astype(bf16)


def prefix_kernel(t_in, kt_in, d_in, rows_in, w_out, p_out):
    here, blocks = t_in.shape[0], t_in.shape[1]
    count = here * SHARE
    row, column = grids()
    eye = jnp.where(row == column, 1.0, 0.0)

    def at(ref, c, e):
        return ref[e // SHARE, c, e % SHARE]

    keys = {
        (c, k): jnp.transpose(whole_of(kt_in[k, c])).astype(bf16)
        for c in range(blocks)
        for k in range(here)
    }
    problems = [(c, e) for c in range(blocks) for e in range(count)]
    scaled = {
        (c, e): (at(t_in, c, e).astype(f32) * at(rows_in, c, e)[1:2]).astype(bf16) for c, e in problems
    }
    for c, e in problems:
        solved = jnp.dot(scaled[c, e], keys[c, e // SHARE], preferred_element_type=f32)
        w_out[e // SHARE, c, e % SHARE] = solved.astype(bf16)
    running = [
        at(rows_in, 0, e)[7:8] * eye - at(d_in, 0, e).astype(f32) for e in range(count)
    ]
    for c in range(1, blocks):
        parts = [x.astype(bf16) for x in running]
        for e in range(count):
            p_out[e // SHARE, c - 1, e % SHARE] = parts[e]
        if c + 1 < blocks:
            running = [
                at(rows_in, c, e)[7:8] * running[e]
                - jnp.dot(at(d_in, c, e), parts[e], preferred_element_type=f32)
                for e in range(count)
            ]


def both_of(left, parts):
    both = jnp.dot(left, jnp.concatenate(parts, axis=1), preferred_element_type=f32)
    half = both.shape[1] // 2
    return both[:, :half] + both[:, half:]


def whole_of(both):
    half = both.shape[1] // 2
    return both[:, :half].astype(f32) + both[:, half:].astype(f32)


def right_from(both):
    return jnp.concatenate([both, both], axis=0)


def value_kernel(groups_count, member, *refs):
    pieces, refs = refs[:groups_count], refs[groups_count:]
    edge, taps, t_in, kt_in, d_in, rows_in, maps, u_out, z_out, span_out, padded, before = refs
    blocks = t_in.shape[1]
    width = pieces[0].shape[1]
    count = width // DV
    ends = edge[...].astype(f32)
    for r in range(SHARE):
        before[:, r * edge.shape[1] : (r + 1) * edge.shape[1]] = ends[4 * r : 4 * r + 4]
    at = pl.multiple_of(pl.program_id(0) * width, 128)
    values = conv_silu(member[0], pieces, before[:, pl.ds(at, width)], taps, padded)
    problems = [(c, e) for c in range(blocks) for e in range(count)]

    def at(ref, c, e):
        return ref[e // SHARE, c, e % SHARE]

    written = {
        (c, e): split(
            jnp.dot(
                at(t_in, c, e),
                values[c * CH : (c + 1) * CH, e * DV : (e + 1) * DV].astype(bf16),
                preferred_element_type=f32,
            )
        )
        for c, e in problems
    }
    tailed = {
        (c, e): (whole_of(kt_in[e // SHARE, c]) * at(rows_in, c, e)[0:1]).astype(bf16)
        for c, e in problems
    }
    adds = {
        pc: jnp.dot(tailed[pc], written[pc][0], preferred_element_type=f32) for pc in problems
    }
    for c, e in problems:
        u_out[e // SHARE, c, e % SHARE] = jnp.concatenate(written[c, e], axis=1)
    running = [adds[0, e] for e in range(count)]
    for c in range(1, blocks):
        parts = [x.astype(bf16) for x in running]
        for e in range(count):
            z_out[e // SHARE, c - 1, e % SHARE] = parts[e]
        running = [
            at(rows_in, c, e)[7:8] * running[e]
            - jnp.dot(at(d_in, c, e), parts[e], preferred_element_type=f32)
            + adds[c, e]
            for e in range(count)
        ]
    for e in range(count):
        span_out[e, :, :DK] = maps[e]
        span_out[e, :, DK:] = running[e].astype(bf16)


def query_kernel(groups_count, heads, member, *refs):
    pieces, refs = refs[:groups_count], refs[groups_count:]
    gate_pieces, refs = refs[:groups_count], refs[groups_count:]
    edge, taps, kt_in, w_in, p_in, u_in, z_in, f_out, g_out, padded, gates = refs
    here = pieces[0].shape[1] // DK
    count = here * SHARE
    blocks = gates.shape[0] // CH
    me = member[0]
    first = pl.program_id(0) * count
    filtered = conv_silu(me, pieces, edge[...].astype(f32)[8:12], taps, padded)
    place_gates(me, gate_pieces, gates, heads, pieces[0].shape[0])
    unit = [unit_rows(filtered[:, k * DK : (k + 1) * DK]) * DK ** (-0.5) for k in range(here)]
    problems = [(c, e) for c in range(blocks) for e in range(count)]
    strengths, rates = strengths_and_rates(gates[...], first, count, heads)
    decays = [decay_terms(rates[c * CH : (c + 1) * CH], count) for c in range(blocks)]

    def at(ref, c, e):
        return right_from(ref[e // SHARE, c, e % SHARE])

    queries = {
        (c, k): unit[k][c * CH : (c + 1) * CH] for c in range(blocks) for k in range(here)
    }
    qk = {
        (c, k): product(as_left(queries[c, k]), right_from(kt_in[k, c])) for c, k in queries
    }
    mix = {(c, e): as_left(qk[c, e // SHARE] * decays[c][0][e]) for c, e in problems}
    entry = {
        (c, e): as_left(
            decays[c][1][e] * queries[c, e // SHARE]
            - jnp.dot(mix[c, e], at(w_in, c, e), preferred_element_type=f32)
        )
        for c, e in problems
    }
    local = {pc: product(mix[pc], at(u_in, *pc)) for pc in problems}
    for c, e in problems:
        here = slice(c * CH, (c + 1) * CH)
        if c == 0:
            f_out[e, here] = entry[c, e][:, :DK]
            g_out[e, here] = local[c, e].astype(bf16)
        else:
            f_out[e, here] = jnp.dot(
                entry[c, e], at(p_in, c - 1, e), preferred_element_type=f32
            ).astype(bf16)
            total = local[c, e] + jnp.dot(
                entry[c, e], at(z_in, c - 1, e), preferred_element_type=f32
            )
            g_out[e, here] = total.astype(bf16)


def handoff_kernel(terms, out):
    spans, heads, width = out.shape[0], out.shape[1], out.shape[3]
    running = [jnp.zeros(out.shape[2:], f32) for h in range(heads)]
    for j in range(spans):
        for h in range(heads):
            out[j, h] = running[h].astype(bf16)
        if j + 1 < spans:
            for h in range(heads):
                erased = jnp.dot(
                    terms[j, h, :, :DK],
                    jnp.concatenate(split(running[h]), axis=1),
                    preferred_element_type=f32,
                )
                erased = erased[:, :width] + erased[:, width:]
                running[h] = running[h] - erased + terms[j, h, :, DK:].astype(f32)


def norm_kernel(count, member, *refs):
    f_in, refs = refs[:count], refs[count:]
    g_in, refs = refs[:count], refs[count:]
    gate, refs = refs[:count], refs[count:]
    state, gain, out = refs
    cells = [(i, h) for i in range(count) for h in range(state.shape[0])]
    core = {
        (i, h): g_in[i][h].astype(f32)
        + jnp.dot(f_in[i][h], state[h], preferred_element_type=f32)
        for i, h in cells
    }
    scale = {
        n: lax.rsqrt(jnp.mean(core[n] * core[n], axis=-1, keepdims=True) + norm_floor)
        for n in cells
    }
    for i, h in cells:
        columns = slice(h * DV, (h + 1) * DV)
        gates = gate[i][:, columns].astype(f32)
        gates = gates / (1.0 + jnp.exp(-gates))
        out[i, :, columns] = (core[i, h] * scale[i, h] * gain[...] * gates).astype(bf16)


def project_kernel(mine, theirs, own_weight, other_weight, kept, *sent):
    rows, depth = mine.shape[0] * mine.shape[1], mine.shape[2]
    product_ = jnp.dot(
        mine[...].reshape(rows, depth), own_weight[...], preferred_element_type=f32
    ) + jnp.dot(theirs[...].reshape(rows, depth), other_weight[...], preferred_element_type=f32)
    size = mine.shape[1]
    kept[...] = product_[:size]
    for i, out in enumerate(sent):
        out[...] = product_[(i + 1) * size : (i + 2) * size].astype(bf16)


def pack_kernel(groups_count, member, *refs):
    array, outs = refs[0], refs[1:]
    me = member[0]
    width = array.shape[1] // groups_count
    for d in range(groups_count):
        at = pl.multiple_of((me ^ d) * width, 128)
        outs[d][...] = array[:, pl.ds(at, width)]


def pack_keys_kernel(groups_count, member, *refs):
    key, value_end, query_end, strength, decay = refs[:5]
    outs = refs[5:]
    me = member[0]
    tokens, width = key.shape[0], key.shape[1] // groups_count
    heads = HV // groups_count
    gates = jnp.concatenate([strength[...], decay[...]], axis=0)
    row = lax.broadcasted_iota(jnp.int32, (2 * heads, 2 * HV), 0)
    column = lax.broadcasted_iota(jnp.int32, (2 * heads, 2 * HV), 1)
    for d in range(groups_count):
        at = me ^ d
        outs[d][:tokens] = key[:, pl.ds(pl.multiple_of(at * width, 128), width)]
        ends = []
        for r in range(SHARE):
            start = pl.multiple_of((at * SHARE + r) * width, 128)
            ends.append(value_end[:, pl.ds(start, width)].astype(f32)[EDGE - 4 :])
        start = pl.multiple_of(at * width, 128)
        ends.append(query_end[:, pl.ds(start, width)].astype(f32)[EDGE - 4 :])
        wanted = jnp.where(row < heads, row, row - heads + HV) + at * heads
        picked = jnp.dot(ones_where(column == wanted), gates, preferred_element_type=f32)
        sets = [picked[4 * i : 4 * i + 4] for i in range(heads // 2)]
        if width > tokens * len(sets):
            sets.append(jnp.zeros((4, width - tokens * len(sets)), f32))
        ends.append(jnp.concatenate(sets, axis=1))
        outs[d][tokens:] = jnp.concatenate(ends, axis=0).astype(bf16)


def shape(dims, kind):
    return jax.ShapeDtypeStruct(dims, kind)


def pack(member, array, groups):
    tokens, width = array.shape[0], array.shape[1] // groups
    return pl.pallas_call(
        functools.partial(pack_kernel, groups),
        grid_spec=grid_of(
            1,
            [pl.BlockSpec(array.shape, lambda p, me: (0, 0))],
            [pl.BlockSpec((tokens, width), lambda p, me: (0, 0))] * groups,
            [],
        ),
        out_shape=[shape((tokens, width), bf16)] * groups,
        compiler_params=params(),
        cost_estimate=cost(3),
        name="pack",
    )(member, array)


def pack_keys(member, key, value, query, strength, decay, groups):
    tokens, width = key.shape[0], key.shape[1] // groups

    def whole(dims):
        return pl.BlockSpec(dims, lambda p, me: (0, 0))

    def end(x):
        return pl.BlockSpec((EDGE, x.shape[1]), lambda p, me: (tokens // EDGE - 1, 0))

    packed = (tokens + EDGE, width)
    return pl.pallas_call(
        functools.partial(pack_keys_kernel, groups),
        grid_spec=grid_of(
            1,
            [whole(key.shape), end(value), end(query), whole(strength.shape), whole(decay.shape)],
            [whole(packed)] * groups,
            [],
        ),
        out_shape=[shape(packed, bf16)] * groups,
        compiler_params=params(),
        cost_estimate=cost(3),
        name="pack_keys",
    )(member, key, value, query, strength, decay)


def per_head(each, dims):
    return pl.BlockSpec((each,) + dims, lambda p, me: (p,) + (0,) * len(dims))


def columns_of(rows, width):
    return pl.BlockSpec((rows, width), lambda p, me: (0, p))


KEY_STEP, VALUE_STEP, PREFIX_STEP, QUERY_STEP = 2, 2, 2, 2


def heads_at_once(key_heads, most):
    return most if key_heads % most == 0 else key_heads


def cost(microseconds):
    return pl.CostEstimate(
        flops=int(microseconds * 1e9), bytes_accessed=int(microseconds * 3e6), transcendentals=0
    )


def grid_of(steps, in_specs, out_specs, scratch):
    return pltpu.PrefetchScalarGridSpec(
        num_scalar_prefetch=1,
        grid=(steps,),
        in_specs=in_specs,
        out_specs=out_specs,
        scratch_shapes=scratch,
    )


def key_terms(member, packed, edge, taps):
    groups = len(packed)
    own = packed[0].shape[0] - EDGE
    tokens = groups * own
    key_heads = taps.shape[1] // DK
    each = heads_at_once(key_heads, KEY_STEP)
    blocks = tokens // CH
    wide = (blocks, SHARE, CH, 2 * CH)
    kinds = [
        (blocks, SHARE, CH, CH),
        (blocks, DK, 2 * CH),
        (blocks, SHARE, DK, DK),
        (blocks, SHARE, 8, CH),
    ]
    types = [bf16] * 3 + [f32]
    return pl.pallas_call(
        functools.partial(key_kernel, groups, key_heads * SHARE),
        grid_spec=grid_of(
            key_heads // each,
            [columns_of(own, each * DK)] * groups
            + [pl.BlockSpec((EDGE, key_heads * DK), lambda p, me: (own // EDGE, 0))] * groups
            + [columns_of(EDGE, each * DK)]
            + [columns_of(taps.shape[0], each * DK)],
            [per_head(each, kind) for kind in kinds]
            + [pl.BlockSpec((each * SHARE, DK, DK), lambda p, me: (p, 0, 0))],
            [pltpu.VMEM((tokens + 8, each * DK), f32), pltpu.VMEM((tokens, 128), bf16)],
        ),
        out_shape=[shape((key_heads,) + kind, t) for kind, t in zip(kinds, types)]
        + [shape((key_heads * SHARE, DK, DK), bf16)],
        compiler_params=params(),
        cost_estimate=cost(12),
        name="key_terms",
    )(member, *packed, *packed, edge, taps)


def value_terms(member, pieces, edge, taps, t_in, kt_in, d_in, rows_in, maps):
    groups = len(pieces)
    own = pieces[0].shape[0]
    tokens = groups * own
    key_heads = t_in.shape[0]
    each = heads_at_once(key_heads, VALUE_STEP)
    blocks = tokens // CH
    width = each * SHARE * DV
    return pl.pallas_call(
        functools.partial(value_kernel, groups),
        grid_spec=grid_of(
            key_heads // each,
            [columns_of(own, width)] * groups
            + [pl.BlockSpec((EDGE, key_heads * DK), lambda p, me: (1, 0))]
            + [columns_of(taps.shape[0], width)]
            + [per_head(each, x.shape[1:]) for x in (t_in, kt_in, d_in, rows_in)]
            + [pl.BlockSpec((each * SHARE, DK, DK), lambda p, me: (p, 0, 0))],
            [
                per_head(each, (blocks, SHARE, CH, 2 * DV)),
                per_head(each, (blocks - 1, SHARE, DK, DV)),
                pl.BlockSpec((each * SHARE, DK, DK + DV), lambda p, me: (p, 0, 0)),
            ],
            [
                pltpu.VMEM((tokens + 8, width), f32),
                pltpu.VMEM((4, key_heads * SHARE * DV), f32),
            ],
        ),
        out_shape=[
            shape((key_heads, blocks, SHARE, CH, 2 * DV), bf16),
            shape((key_heads, blocks - 1, SHARE, DK, DV), bf16),
            shape((key_heads * SHARE, DK, DK + DV), bf16),
        ],
        compiler_params=params(),
        cost_estimate=cost(7),
        name="value_terms",
    )(member, *pieces, edge, taps, t_in, kt_in, d_in, rows_in, maps)


def query_terms(member, pieces, edge, packed, taps, kt, w, p, u, z):
    groups = len(pieces)
    own = pieces[0].shape[0]
    tokens = groups * own
    key_heads = kt.shape[0]
    each = heads_at_once(key_heads, QUERY_STEP)
    out = pl.BlockSpec((each * SHARE, tokens, DK), lambda p, me: (p, 0, 0))
    return pl.pallas_call(
        functools.partial(query_kernel, groups, key_heads * SHARE),
        grid_spec=grid_of(
            key_heads // each,
            [columns_of(own, each * DK)] * groups
            + [pl.BlockSpec((EDGE, key_heads * DK), lambda p, me: (own // EDGE, 0))] * groups
            + [pl.BlockSpec((EDGE, each * DK), lambda p, me: (1, p))]
            + [columns_of(taps.shape[0], each * DK)]
            + [per_head(each, x.shape[1:]) for x in (kt, w, p, u, z)],
            [out, out],
            [pltpu.VMEM((tokens + 8, each * DK), f32), pltpu.VMEM((tokens, 128), bf16)],
        ),
        out_shape=[shape((key_heads * SHARE, tokens, DK), bf16)] * 2,
        compiler_params=params(),
        cost_estimate=cost(9),
        name="query_terms",
    )(member, *pieces, *packed, edge, taps, kt, w, p, u, z)


def handoff(terms):
    dims = terms.shape[:3] + (terms.shape[3] - DK,)
    return pl.pallas_call(
        handoff_kernel,
        out_shape=shape(dims, bf16),
        compiler_params=params(16),
        cost_estimate=cost(1),
        name="handoff",
    )(terms)


def prefix_terms(t, kt, d, rows):
    key_heads, blocks = t.shape[0], t.shape[1]
    each = heads_at_once(key_heads, PREFIX_STEP)

    def some(dims):
        return pl.BlockSpec((each,) + dims, lambda p: (p,) + (0,) * len(dims))

    outs = [(blocks, SHARE, CH, DK), (blocks - 1, SHARE, DK, DK)]
    return pl.pallas_call(
        prefix_kernel,
        grid=(key_heads // each,),
        in_specs=[some(x.shape[1:]) for x in (t, kt, d, rows)],
        out_specs=[some(dims) for dims in outs],
        out_shape=[shape((key_heads,) + dims, bf16) for dims in outs],
        compiler_params=params(),
        cost_estimate=cost(5),
        name="prefix_terms",
    )(t, kt, d, rows)


def normed_rows(member, f, g, state, gate, gain, parity):
    heads = state.shape[0]
    count = len(gate)
    size, width = gate[0].shape

    def token_block(i):
        return pl.BlockSpec(
            (heads, size, DK), lambda p, me: (0, me[0] ^ (2 * i + parity), 0)
        )

    whole = pl.BlockSpec((size, width), lambda p, me: (0, 0))
    return pl.pallas_call(
        functools.partial(norm_kernel, count),
        grid_spec=grid_of(
            1,
            [token_block(i) for i in range(count)] * 2
            + [whole] * count
            + [
                pl.BlockSpec((heads, DK, DV), lambda p, me: (0, 0, 0)),
                pl.BlockSpec((1, DV), lambda p, me: (0, 0)),
            ],
            pl.BlockSpec((count, size, width), lambda p, me: (0, 0, 0)),
            [],
        ),
        out_shape=shape((count, size, width), bf16),
        compiler_params=params(16),
        cost_estimate=cost(1),
        name="normed_rows",
    )(member, *([f] * count), *([g] * count), *gate, state, gain)


def projected(mine, theirs, own_weight, other_weight, start, width):
    ranks, size, depth = mine.shape
    tile = min(width, 512)
    whole = pl.BlockSpec((ranks, size, depth), lambda j: (0, 0, 0))
    weight = pl.BlockSpec((depth, tile), lambda j: (0, j + start // tile))
    out = pl.BlockSpec((size, tile), lambda j: (0, j))
    return pl.pallas_call(
        project_kernel,
        grid=(width // tile,),
        in_specs=[whole, whole, weight, weight],
        out_specs=[out] * ranks,
        out_shape=[shape((size, width), f32)] + [shape((size, width), bf16)] * (ranks - 1),
        compiler_params=params(16),
        cost_estimate=cost(3),
        name="projected",
    )(mine, theirs, own_weight, other_weight)


def sum_kernel(cuts, *refs):
    parts, out = refs[:-1], refs[-1]
    each = len(parts) // cuts
    for cut in range(cuts):
        total = parts[cut * each][...]
        for part in parts[cut * each + 1 : (cut + 1) * each]:
            total = total + part[...].astype(f32)
        width = total.shape[1]
        out[:, cut * width : (cut + 1) * width] = total.astype(bf16)


def summed_parts(parts, cuts):
    rows, width = parts[0].shape
    return pl.pallas_call(
        functools.partial(sum_kernel, cuts),
        out_shape=shape((rows, width * cuts), bf16),
        compiler_params=params(16),
        cost_estimate=cost(1),
        name="summed_parts",
    )(*parts)


def to_members(pieces):
    groups = len(pieces)
    return [pieces[0]] + [
        lax.ppermute(pieces[d], "head", [(i, i ^ d) for i in range(groups)])
        for d in range(1, groups)
    ]


def after_all(values, others):
    return lax.optimization_barrier((*values, *others))[: len(values)]


def to_runners(terms):
    spans = lax.axis_size("seq")
    heads = terms.shape[0]
    if spans <= heads:
        pieces = terms.reshape(spans, heads // spans, DK, DK + DV)
    else:
        cuts = spans // heads
        maps = jnp.repeat(terms[:, :, :DK], cuts, axis=0)
        adds = terms[:, :, DK:].reshape(heads, DK, cuts, DV // cuts)
        adds = adds.transpose(0, 2, 1, 3).reshape(spans, DK, DV // cuts)
        pieces = jnp.concatenate([maps, adds], axis=2)[:, None]
    return lax.all_to_all(pieces, "seq", 0, 0)


def from_runners(entries, heads):
    spans, each, depth, width = entries.shape
    entries = lax.all_to_all(entries, "seq", 0, 0)
    entries = entries.reshape(heads // each, DV // width, each, depth, width)
    return entries.transpose(0, 2, 3, 1, 4).reshape(heads, depth, DV)


def on_device(
    query_input,
    key_input,
    value_input,
    gate_input,
    write_strength,
    log_decay,
    filter_query,
    filter_key,
    filter_value,
    norm_gain,
    out_weight,
):
    groups = lax.axis_size("head")
    spans = lax.axis_size("seq")
    member = lax.axis_index("head").astype(jnp.int32).reshape(1)
    heads = filter_value.shape[1] // DV

    key_out = pack_keys(
        member, key_input, value_input, query_input, write_strength.T, log_decay.T, groups
    )
    packed = to_members(key_out)
    edge = packed[0][-2 * EDGE :]
    for d in range(1, groups):
        edge = jnp.where((member[0] ^ d) == groups - 1, packed[d][-2 * EDGE :], edge)
    edge = jnp.where(lax.axis_index("seq") == spans - 1, jnp.zeros_like(edge), edge)
    value_out = pack(member, value_input, groups)
    query_out = pack(member, query_input, groups)
    gate_out = pack(member, gate_input, groups)
    edge, *value_out = after_all([edge, *value_out], [*query_out, *gate_out])
    edge = lax.ppermute(edge, "seq", [(s, (s + 1) % spans) for s in range(spans)])
    value_rows = to_members(value_out)
    t, kt, d, rows, maps = key_terms(member, packed, edge, filter_key)
    u, z, adds = value_terms(member, value_rows, edge, filter_value, t, kt, d, rows, maps)
    query_rows = to_members(after_all(query_out, [adds]))
    gate_rows = to_members(after_all(gate_out, [adds]))
    swap = [(i, i ^ 1) for i in range(groups)]
    (own_weight,) = after_all([out_weight], [adds])
    other_weight = lax.ppermute(own_weight, "head", swap)
    w, p = prefix_terms(*after_all([t, kt, d, rows], [adds]))
    adds, w, p = after_all([to_runners(adds), w, p], [])
    entries = handoff(adds)
    query_rows = after_all(query_rows, [entries, *gate_rows])
    f, g = query_terms(member, query_rows, edge, packed, filter_query, kt, w, p, u, z)
    state = from_runners(entries, heads)

    gain = norm_gain.reshape(1, DV)
    theirs = normed_rows(member, f, g, state, gate_rows[1::2], gain, 1)
    theirs = lax.ppermute(theirs, "head", swap)
    mine = normed_rows(member, f, g, state, gate_rows[0::2], gain, 0)
    width = out_weight.shape[1]
    cuts = 2
    parts = []
    for cut in range(cuts):
        kept, *sent = projected(
            mine, theirs, out_weight, other_weight, cut * width // cuts, width // cuts
        )
        parts.append(kept)
        parts += [
            lax.ppermute(part, "head", [(i, i ^ (2 * step + 2)) for i in range(groups)])
            for step, part in enumerate(sent)
        ]
    return summed_parts(parts, cuts)


def solution(mesh):
    tokens = P(("seq", "head"), None)
    placed = (tokens,) * 6 + (P(None, "head"),) * 3 + (P(), P("head", None))
    return jax.shard_map(
        on_device, mesh=mesh, in_specs=placed, out_specs=tokens, check_vma=False
    )
```

```python
import functools

import jax
import jax.numpy as jnp
from jax import lax
from jax.experimental import pallas as pl
from jax.experimental.pallas import tpu as pltpu
from jax.sharding import PartitionSpec as P

HK = 16
HV = 32
DK = 128
DV = 128
CH = 128
EDGE = 16
SHARE = HV // HK
ODD_ROWS = 16

norm_floor = 1e-06
f32 = jnp.float32
bf16 = jnp.bfloat16


def params(megabytes=60):
    return pltpu.CompilerParams(vmem_limit_bytes=megabytes * 1024 * 1024)


def split(x):
    high = x.astype(bf16)
    return high, (x - high.astype(f32)).astype(bf16)


def as_left(x):
    return jnp.concatenate(split(x), axis=1)


def right_of(high, low):
    row = jnp.concatenate([high, low], axis=1)
    return jnp.concatenate([row, row], axis=0)


def as_right(x):
    return right_of(*split(x))


def product(left, right):
    both = jnp.dot(left, right, preferred_element_type=f32)
    half = both.shape[1] // 2
    return both[:, :half] + both[:, half:]


def grids():
    row = lax.broadcasted_iota(jnp.int32, (CH, CH), 0)
    column = lax.broadcasted_iota(jnp.int32, (CH, CH), 1)
    return row, column


def ones_where(mask):
    return jnp.where(mask, 1.0, 0.0).astype(bf16)


def place(me, pieces, out, margin):
    size = pieces[0].shape[0]
    for d, piece in enumerate(pieces):
        at = pl.multiple_of((me ^ d) * size + margin, 8)
        out[pl.ds(at, size), :] = piece[...].astype(out.dtype)


def place_gates(me, pieces, out, heads, size):
    for d, piece in enumerate(pieces):
        ends = piece[...].astype(f32)[12:16]
        sets = [ends[:, i * size : (i + 1) * size] for i in range(heads // 2)]
        rows = jnp.concatenate(sets + [jnp.zeros((128 - 2 * heads, size), f32)], axis=0)
        at = pl.multiple_of((me ^ d) * size, 16)
        out[pl.ds(at, size), :] = jnp.transpose(rows).astype(bf16)


def conv_silu(me, pieces, edge, taps_ref, padded):
    length = padded.shape[0] - 8
    taps = taps_ref[...].astype(f32)
    padded[8 - edge.shape[0] : 8] = edge
    place(me, pieces, padded, 8)
    margin = taps.shape[0] - 1
    summed = taps[margin : margin + 1] * padded[8 : 8 + length]
    for offset in range(margin):
        start = 8 - margin + offset
        summed = summed + taps[offset : offset + 1] * padded[start : start + length]
    return summed / (1.0 + jnp.exp(-summed))


def unit_rows(field):
    return field * lax.rsqrt(jnp.sum(field * field, axis=-1, keepdims=True) + norm_floor)


def strengths_and_rates(gates, first, count, heads):
    lane = lax.broadcasted_iota(jnp.int32, (gates.shape[1], CH), 0)
    picks = [ones_where(lane == first + e) for e in range(count)]
    picks += [ones_where(lane == heads + first + e) for e in range(count)]
    picked = jnp.dot(gates, jnp.concatenate(picks, axis=1), preferred_element_type=f32)
    return picked[:, : count * CH], picked[:, count * CH :].astype(bf16)


def decay_terms(rates, count, with_growth=True):
    row, column = grids()
    below = ones_where(column <= row)
    pieces = []
    for e in range(count):
        rate = rates[:, e * CH : (e + 1) * CH]
        pieces.append(jnp.where(row > column, rate, jnp.zeros_like(rate)))
    if with_growth:
        pieces.append(rates)
    sums = jnp.dot(below, jnp.concatenate(pieces, axis=1), preferred_element_type=f32)
    ratios, growth = [], []
    for e in range(count):
        at = e * CH
        ratios.append(jnp.where(column <= row, jnp.exp(sums[:, at : at + CH]), 0.0))
        if with_growth:
            at += count * CH
            growth.append(jnp.exp(sums[:, at : at + CH]))
    return ratios, growth


def unit_lower_inverses(lower):
    row, column = grids()
    names = list(lower)
    eye = jnp.where(row == column, 1.0, 0.0)
    pair = (row // 2 == column // 2) & (column < row)
    halves = {n: split(lower[n]) for n in names}
    inverse = {n: eye - jnp.where(pair, lower[n], 0.0) for n in names}
    size = 2
    while size < CH:
        mask = ones_where(
            (row // (2 * size) == column // (2 * size))
            & ((row // size) % 2 == 1)
            & ((column // size) % 2 == 0)
        )
        rounded = {n: inverse[n].astype(bf16) for n in names}
        if size < ODD_ROWS:
            first = {
                n: jnp.dot(halves[n][0] * mask, rounded[n], preferred_element_type=f32).astype(bf16)
                for n in names
            }
            for n in names:
                inverse[n] = inverse[n] - jnp.dot(rounded[n], first[n], preferred_element_type=f32)
        else:
            starts = range(size, CH, 2 * size)

            def odd(x):
                return jnp.concatenate([x[s : s + size] for s in starts], axis=0)

            def back(x, even):
                rows = []
                for i, s in enumerate(starts):
                    rows += [even[s - size : s], x[i * size : (i + 1) * size]]
                return jnp.concatenate(rows, axis=0)

            some = odd(mask)
            nothing = jnp.zeros((CH, CH), bf16)
            first = {
                n: jnp.dot(
                    odd(halves[n][0]) * some, rounded[n], preferred_element_type=f32
                ).astype(bf16)
                for n in names
            }
            for n in names:
                change = jnp.dot(
                    odd(rounded[n]), back(first[n], nothing), preferred_element_type=f32
                )
                inverse[n] = back(odd(inverse[n]) - change, inverse[n])
        size *= 2
    parts = {n: split(inverse[n]) for n in names}
    left = {
        n: (
            eye
            - inverse[n]
            - product(jnp.concatenate(halves[n], axis=1), right_of(*parts[n]))
        ).astype(bf16)
        for n in names
    }
    return {
        n: inverse[n] + jnp.dot(parts[n][0], left[n], preferred_element_type=f32) for n in names
    }


def key_kernel(groups_count, heads, member, *refs):
    pieces, refs = refs[:groups_count], refs[groups_count:]
    gate_pieces, refs = refs[:groups_count], refs[groups_count:]
    edge, taps, t_out, kt_out, d_out, rows_out, map_out, padded, gates = refs
    here = pieces[0].shape[1] // DK
    count = here * SHARE
    blocks = gates.shape[0] // CH
    me = member[0]
    first = pl.program_id(0) * count
    filtered = conv_silu(me, pieces, edge[...].astype(f32)[EDGE - 8 :], taps, padded)
    place_gates(me, gate_pieces, gates, heads, pieces[0].shape[0])
    row, column = grids()
    eye = jnp.where(row == column, 1.0, 0.0)
    groups = [(c, k) for c in range(blocks) for k in range(here)]
    problems = [(c, e) for c in range(blocks) for e in range(count)]

    def chunk_of(x, c):
        return x[c * CH : (c + 1) * CH]

    strengths, rates = strengths_and_rates(gates[...], first, count, heads)
    unit = [unit_rows(filtered[:, k * DK : (k + 1) * DK]) for k in range(here)]
    ratio = [decay_terms(chunk_of(rates, c), count, False)[0] for c in range(blocks)]
    keys = {(c, k): chunk_of(unit[k], c) for c, k in groups}
    turned = {g: jnp.transpose(keys[g]) for g in groups}
    sides = {g: split(turned[g]) for g in groups}
    kk = {g: product(as_left(keys[g]), right_of(*sides[g])) for g in groups}
    lane = lax.broadcasted_iota(jnp.int32, (2 * count, gates.shape[1]), 1)
    order = lax.broadcasted_iota(jnp.int32, (2 * count, gates.shape[1]), 0)
    pick = ones_where(lane == first + jnp.where(order < count, order, order - count + heads))
    across = [
        lax.dot_general(
            pick,
            gates[c * CH : (c + 1) * CH, :],
            (((1,), (1,)), ((), ())),
            preferred_element_type=f32,
        )
        for c in range(blocks)
    ]
    growing = [
        jnp.exp(
            jnp.dot(across[c].astype(bf16), ones_where(row <= column), preferred_element_type=f32)
        )
        for c in range(blocks)
    ]
    lower, ktail, ends = {}, {}, {}
    for c, k in groups:
        kt_out[k, c] = jnp.concatenate(sides[c, k], axis=1)
    for c, e in problems:
        ratios = ratio[c][e]
        strength = chunk_of(strengths, c)[:, e * CH : (e + 1) * CH]
        k = e // SHARE
        lower[c, e] = jnp.where(column < row, strength * kk[c, k] * ratios, 0.0)
        ktail[c, e] = (turned[c, k] * ratios[CH - 1 : CH]).astype(bf16)
        growth = growing[c][count + e : count + e + 1]
        ends[c, e] = jnp.broadcast_to(growth[:, CH - 1 : CH], (1, CH))
        rows_out[k, c, e % SHARE] = jnp.concatenate(
            [ratios[CH - 1 : CH], growth] + [ends[c, e]] * 6, axis=0
        )
    inverse = unit_lower_inverses(lower)
    solving = {
        (c, e): (inverse[c, e] * across[c][e : e + 1]).astype(bf16) for c, e in problems
    }
    rounded = {g: keys[g].astype(bf16) for g in groups}
    solved = {
        (c, e): jnp.dot(
            (
                inverse[c, e]
                * (across[c][e : e + 1] * growing[c][count + e : count + e + 1])
            ).astype(bf16),
            rounded[c, e // SHARE],
            preferred_element_type=f32,
        ).astype(bf16)
        for c, e in problems
    }
    maps = {
        pc: jnp.dot(ktail[pc], solved[pc], preferred_element_type=f32).astype(bf16)
        for pc in problems
    }
    for c, e in problems:
        k = e // SHARE
        t_out[k, c, e % SHARE] = solving[c, e]
        d_out[k, c, e % SHARE] = maps[c, e]
    running = [
        ends[0, e] * eye - maps[0, e].astype(f32) for e in range(count)
    ]
    for c in range(1, blocks):
        running = [
            ends[c, e] * running[e]
            - jnp.dot(maps[c, e], running[e].astype(bf16), preferred_element_type=f32)
            for e in range(count)
        ]
    for e in range(count):
        map_out[e] = (eye - running[e]).astype(bf16)


def prefix_kernel(t_in, kt_in, d_in, rows_in, w_out, p_out):
    here, blocks = t_in.shape[0], t_in.shape[1]
    count = here * SHARE
    row, column = grids()
    eye = jnp.where(row == column, 1.0, 0.0)

    def at(ref, c, e):
        return ref[e // SHARE, c, e % SHARE]

    keys = {
        (c, k): jnp.transpose(whole_of(kt_in[k, c])).astype(bf16)
        for c in range(blocks)
        for k in range(here)
    }
    problems = [(c, e) for c in range(blocks) for e in range(count)]
    scaled = {
        (c, e): (at(t_in, c, e).astype(f32) * at(rows_in, c, e)[1:2]).astype(bf16) for c, e in problems
    }
    for c, e in problems:
        solved = jnp.dot(scaled[c, e], keys[c, e // SHARE], preferred_element_type=f32)
        w_out[e // SHARE, c, e % SHARE] = solved.astype(bf16)
    running = [
        at(rows_in, 0, e)[7:8] * eye - at(d_in, 0, e).astype(f32) for e in range(count)
    ]
    for c in range(1, blocks):
        parts = [x.astype(bf16) for x in running]
        for e in range(count):
            p_out[e // SHARE, c - 1, e % SHARE] = parts[e]
        if c + 1 < blocks:
            running = [
                at(rows_in, c, e)[7:8] * running[e]
                - jnp.dot(at(d_in, c, e), parts[e], preferred_element_type=f32)
                for e in range(count)
            ]


def both_of(left, parts):
    both = jnp.dot(left, jnp.concatenate(parts, axis=1), preferred_element_type=f32)
    half = both.shape[1] // 2
    return both[:, :half] + both[:, half:]


def whole_of(both):
    half = both.shape[1] // 2
    return both[:, :half].astype(f32) + both[:, half:].astype(f32)


def right_from(both):
    return jnp.concatenate([both, both], axis=0)


def value_kernel(groups_count, member, *refs):
    pieces, refs = refs[:groups_count], refs[groups_count:]
    edge, taps, t_in, kt_in, d_in, rows_in, maps, u_out, z_out, span_out, padded, before = refs
    blocks = t_in.shape[1]
    width = pieces[0].shape[1]
    count = width // DV
    ends = edge[...].astype(f32)
    for r in range(SHARE):
        before[:, r * edge.shape[1] : (r + 1) * edge.shape[1]] = ends[4 * r : 4 * r + 4]
    at = pl.multiple_of(pl.program_id(0) * width, 128)
    values = conv_silu(member[0], pieces, before[:, pl.ds(at, width)], taps, padded)
    problems = [(c, e) for c in range(blocks) for e in range(count)]

    def at(ref, c, e):
        return ref[e // SHARE, c, e % SHARE]

    written = {
        (c, e): split(
            jnp.dot(
                at(t_in, c, e),
                values[c * CH : (c + 1) * CH, e * DV : (e + 1) * DV].astype(bf16),
                preferred_element_type=f32,
            )
        )
        for c, e in problems
    }
    tailed = {
        (c, e): (whole_of(kt_in[e // SHARE, c]) * at(rows_in, c, e)[0:1]).astype(bf16)
        for c, e in problems
    }
    adds = {
        pc: jnp.dot(tailed[pc], written[pc][0], preferred_element_type=f32) for pc in problems
    }
    for c, e in problems:
        u_out[e // SHARE, c, e % SHARE] = jnp.concatenate(written[c, e], axis=1)
    running = [adds[0, e] for e in range(count)]
    for c in range(1, blocks):
        parts = [x.astype(bf16) for x in running]
        for e in range(count):
            z_out[e // SHARE, c - 1, e % SHARE] = parts[e]
        running = [
            at(rows_in, c, e)[7:8] * running[e]
            - jnp.dot(at(d_in, c, e), parts[e], preferred_element_type=f32)
            + adds[c, e]
            for e in range(count)
        ]
    for e in range(count):
        span_out[e, :, :DK] = maps[e]
        span_out[e, :, DK:] = running[e].astype(bf16)


def query_kernel(groups_count, heads, member, *refs):
    pieces, refs = refs[:groups_count], refs[groups_count:]
    gate_pieces, refs = refs[:groups_count], refs[groups_count:]
    edge, taps, kt_in, w_in, p_in, u_in, z_in, out, padded, gates = refs
    here = pieces[0].shape[1] // DK
    count = here * SHARE
    blocks = gates.shape[0] // CH
    me = member[0]
    first = pl.program_id(0) * count
    filtered = conv_silu(me, pieces, edge[...].astype(f32)[8:12], taps, padded)
    place_gates(me, gate_pieces, gates, heads, pieces[0].shape[0])
    unit = [unit_rows(filtered[:, k * DK : (k + 1) * DK]) * DK ** (-0.5) for k in range(here)]
    problems = [(c, e) for c in range(blocks) for e in range(count)]
    strengths, rates = strengths_and_rates(gates[...], first, count, heads)
    decays = [decay_terms(rates[c * CH : (c + 1) * CH], count) for c in range(blocks)]

    def at(ref, c, e):
        return right_from(ref[e // SHARE, c, e % SHARE])

    queries = {
        (c, k): unit[k][c * CH : (c + 1) * CH] for c in range(blocks) for k in range(here)
    }
    qk = {
        (c, k): product(as_left(queries[c, k]), right_from(kt_in[k, c])) for c, k in queries
    }
    mix = {(c, e): as_left(qk[c, e // SHARE] * decays[c][0][e]) for c, e in problems}
    entry = {
        (c, e): as_left(
            decays[c][1][e] * queries[c, e // SHARE]
            - jnp.dot(mix[c, e], at(w_in, c, e), preferred_element_type=f32)
        )
        for c, e in problems
    }
    local = {pc: product(mix[pc], at(u_in, *pc)) for pc in problems}
    for c, e in problems:
        here = slice(c * CH, (c + 1) * CH)
        if c == 0:
            out[e, here, :DK] = entry[c, e][:, :DK]
            out[e, here, DK:] = local[c, e].astype(bf16)
        else:
            out[e, here, :DK] = jnp.dot(
                entry[c, e], at(p_in, c - 1, e), preferred_element_type=f32
            ).astype(bf16)
            later = jnp.dot(entry[c, e], at(z_in, c - 1, e), preferred_element_type=f32)
            out[e, here, DK:] = (local[c, e] + later).astype(bf16)


def handoff_kernel(terms, out):
    spans, heads, width = out.shape[0], out.shape[1], out.shape[3]
    running = [jnp.zeros(out.shape[2:], f32) for h in range(heads)]
    for j in range(spans):
        for h in range(heads):
            out[j, h] = running[h].astype(bf16)
        if j + 1 < spans:
            for h in range(heads):
                erased = jnp.dot(
                    terms[j, h, :, :DK],
                    jnp.concatenate(split(running[h]), axis=1),
                    preferred_element_type=f32,
                )
                erased = erased[:, :width] + erased[:, width:]
                running[h] = running[h] - erased + terms[j, h, :, DK:].astype(f32)


def norm_kernel(count, member, *refs):
    terms, refs = refs[:count], refs[count:]
    gate, refs = refs[:count], refs[count:]
    state, gain, out = refs
    cells = [(i, h) for i in range(count) for h in range(state.shape[0])]
    core = {
        (i, h): terms[i][h, :, DK:].astype(f32)
        + jnp.dot(terms[i][h, :, :DK], state[h], preferred_element_type=f32)
        for i, h in cells
    }
    scale = {
        n: lax.rsqrt(jnp.mean(core[n] * core[n], axis=-1, keepdims=True) + norm_floor)
        for n in cells
    }
    for i, h in cells:
        columns = slice(h * DV, (h + 1) * DV)
        gates = gate[i][:, columns].astype(f32)
        gates = gates / (1.0 + jnp.exp(-gates))
        out[i, :, columns] = (core[i, h] * scale[i, h] * gain[...] * gates).astype(bf16)


def project_kernel(mine, theirs, own_weight, other_weight, kept, *sent):
    rows, depth = mine.shape[0] * mine.shape[1], mine.shape[2]
    product_ = jnp.dot(
        mine[...].reshape(rows, depth), own_weight[...], preferred_element_type=f32
    ) + jnp.dot(theirs[...].reshape(rows, depth), other_weight[...], preferred_element_type=f32)
    size = mine.shape[1]
    kept[...] = product_[:size]
    for i, out in enumerate(sent):
        out[...] = product_[(i + 1) * size : (i + 2) * size].astype(bf16)


def pack_kernel(groups_count, member, *refs):
    array, outs = refs[0], refs[1:]
    me = member[0]
    width = array.shape[1] // groups_count
    for d in range(groups_count):
        at = pl.multiple_of((me ^ d) * width, 128)
        outs[d][...] = array[:, pl.ds(at, width)]


def pack_keys_kernel(groups_count, member, *refs):
    key, value_end, query_end, strength, decay = refs[:5]
    outs = refs[5:]
    me = member[0]
    tokens, width = key.shape[0], key.shape[1] // groups_count
    heads = HV // groups_count
    gates = jnp.concatenate([strength[...], decay[...]], axis=0)
    row = lax.broadcasted_iota(jnp.int32, (2 * heads, 2 * HV), 0)
    column = lax.broadcasted_iota(jnp.int32, (2 * heads, 2 * HV), 1)
    for d in range(groups_count):
        at = me ^ d
        outs[d][:tokens] = key[:, pl.ds(pl.multiple_of(at * width, 128), width)]
        ends = []
        for r in range(SHARE):
            start = pl.multiple_of((at * SHARE + r) * width, 128)
            ends.append(value_end[:, pl.ds(start, width)].astype(f32)[EDGE - 4 :])
        start = pl.multiple_of(at * width, 128)
        ends.append(query_end[:, pl.ds(start, width)].astype(f32)[EDGE - 4 :])
        wanted = jnp.where(row < heads, row, row - heads + HV) + at * heads
        picked = jnp.dot(ones_where(column == wanted), gates, preferred_element_type=f32)
        sets = [picked[4 * i : 4 * i + 4] for i in range(heads // 2)]
        if width > tokens * len(sets):
            sets.append(jnp.zeros((4, width - tokens * len(sets)), f32))
        ends.append(jnp.concatenate(sets, axis=1))
        outs[d][tokens:] = jnp.concatenate(ends, axis=0).astype(bf16)


def shape(dims, kind):
    return jax.ShapeDtypeStruct(dims, kind)


def pack(member, array, groups):
    tokens, width = array.shape[0], array.shape[1] // groups
    return pl.pallas_call(
        functools.partial(pack_kernel, groups),
        grid_spec=grid_of(
            1,
            [pl.BlockSpec(array.shape, lambda p, me: (0, 0))],
            [pl.BlockSpec((tokens, width), lambda p, me: (0, 0))] * groups,
            [],
        ),
        out_shape=[shape((tokens, width), bf16)] * groups,
        compiler_params=params(),
        cost_estimate=cost(3),
        name="pack",
    )(member, array)


def pack_keys(member, key, value, query, strength, decay, groups):
    tokens, width = key.shape[0], key.shape[1] // groups

    def whole(dims):
        return pl.BlockSpec(dims, lambda p, me: (0, 0))

    def end(x):
        return pl.BlockSpec((EDGE, x.shape[1]), lambda p, me: (tokens // EDGE - 1, 0))

    packed = (tokens + EDGE, width)
    return pl.pallas_call(
        functools.partial(pack_keys_kernel, groups),
        grid_spec=grid_of(
            1,
            [whole(key.shape), end(value), end(query), whole(strength.shape), whole(decay.shape)],
            [whole(packed)] * groups,
            [],
        ),
        out_shape=[shape(packed, bf16)] * groups,
        compiler_params=params(),
        cost_estimate=cost(3),
        name="pack_keys",
    )(member, key, value, query, strength, decay)


def per_head(each, dims):
    return pl.BlockSpec((each,) + dims, lambda p, me: (p,) + (0,) * len(dims))


def columns_of(rows, width):
    return pl.BlockSpec((rows, width), lambda p, me: (0, p))


KEY_STEP, VALUE_STEP, PREFIX_STEP, QUERY_STEP = 2, 2, 2, 2


def heads_at_once(key_heads, most):
    return most if key_heads % most == 0 else key_heads


def cost(microseconds):
    return pl.CostEstimate(
        flops=int(microseconds * 1e9), bytes_accessed=int(microseconds * 3e6), transcendentals=0
    )


def grid_of(steps, in_specs, out_specs, scratch):
    return pltpu.PrefetchScalarGridSpec(
        num_scalar_prefetch=1,
        grid=(steps,),
        in_specs=in_specs,
        out_specs=out_specs,
        scratch_shapes=scratch,
    )


def key_terms(member, packed, edge, taps):
    groups = len(packed)
    own = packed[0].shape[0] - EDGE
    tokens = groups * own
    key_heads = taps.shape[1] // DK
    each = heads_at_once(key_heads, KEY_STEP)
    blocks = tokens // CH
    wide = (blocks, SHARE, CH, 2 * CH)
    kinds = [
        (blocks, SHARE, CH, CH),
        (blocks, DK, 2 * CH),
        (blocks, SHARE, DK, DK),
        (blocks, SHARE, 8, CH),
    ]
    types = [bf16] * 3 + [f32]
    return pl.pallas_call(
        functools.partial(key_kernel, groups, key_heads * SHARE),
        grid_spec=grid_of(
            key_heads // each,
            [columns_of(own, each * DK)] * groups
            + [pl.BlockSpec((EDGE, key_heads * DK), lambda p, me: (own // EDGE, 0))] * groups
            + [columns_of(EDGE, each * DK)]
            + [columns_of(taps.shape[0], each * DK)],
            [per_head(each, kind) for kind in kinds]
            + [pl.BlockSpec((each * SHARE, DK, DK), lambda p, me: (p, 0, 0))],
            [pltpu.VMEM((tokens + 8, each * DK), f32), pltpu.VMEM((tokens, 128), bf16)],
        ),
        out_shape=[shape((key_heads,) + kind, t) for kind, t in zip(kinds, types)]
        + [shape((key_heads * SHARE, DK, DK), bf16)],
        compiler_params=params(),
        cost_estimate=cost(12),
        name="key_terms",
    )(member, *packed, *packed, edge, taps)


def value_terms(member, pieces, edge, taps, t_in, kt_in, d_in, rows_in, maps):
    groups = len(pieces)
    own = pieces[0].shape[0]
    tokens = groups * own
    key_heads = t_in.shape[0]
    each = heads_at_once(key_heads, VALUE_STEP)
    blocks = tokens // CH
    width = each * SHARE * DV
    return pl.pallas_call(
        functools.partial(value_kernel, groups),
        grid_spec=grid_of(
            key_heads // each,
            [columns_of(own, width)] * groups
            + [pl.BlockSpec((EDGE, key_heads * DK), lambda p, me: (1, 0))]
            + [columns_of(taps.shape[0], width)]
            + [per_head(each, x.shape[1:]) for x in (t_in, kt_in, d_in, rows_in)]
            + [pl.BlockSpec((each * SHARE, DK, DK), lambda p, me: (p, 0, 0))],
            [
                per_head(each, (blocks, SHARE, CH, 2 * DV)),
                per_head(each, (blocks - 1, SHARE, DK, DV)),
                pl.BlockSpec((each * SHARE, DK, DK + DV), lambda p, me: (p, 0, 0)),
            ],
            [
                pltpu.VMEM((tokens + 8, width), f32),
                pltpu.VMEM((4, key_heads * SHARE * DV), f32),
            ],
        ),
        out_shape=[
            shape((key_heads, blocks, SHARE, CH, 2 * DV), bf16),
            shape((key_heads, blocks - 1, SHARE, DK, DV), bf16),
            shape((key_heads * SHARE, DK, DK + DV), bf16),
        ],
        compiler_params=params(),
        cost_estimate=cost(7),
        name="value_terms",
    )(member, *pieces, edge, taps, t_in, kt_in, d_in, rows_in, maps)


def query_terms(member, pieces, edge, packed, taps, kt, w, p, u, z):
    groups = len(pieces)
    own = pieces[0].shape[0]
    tokens = groups * own
    key_heads = kt.shape[0]
    each = heads_at_once(key_heads, QUERY_STEP)
    out = pl.BlockSpec((each * SHARE, tokens, DK + DV), lambda p, me: (p, 0, 0))
    return pl.pallas_call(
        functools.partial(query_kernel, groups, key_heads * SHARE),
        grid_spec=grid_of(
            key_heads // each,
            [columns_of(own, each * DK)] * groups
            + [pl.BlockSpec((EDGE, key_heads * DK), lambda p, me: (own // EDGE, 0))] * groups
            + [pl.BlockSpec((EDGE, each * DK), lambda p, me: (1, p))]
            + [columns_of(taps.shape[0], each * DK)]
            + [per_head(each, x.shape[1:]) for x in (kt, w, p, u, z)],
            out,
            [pltpu.VMEM((tokens + 8, each * DK), f32), pltpu.VMEM((tokens, 128), bf16)],
        ),
        out_shape=shape((key_heads * SHARE, tokens, DK + DV), bf16),
        compiler_params=params(),
        cost_estimate=cost(9),
        name="query_terms",
    )(member, *pieces, *packed, edge, taps, kt, w, p, u, z)


def handoff(terms):
    dims = terms.shape[:3] + (terms.shape[3] - DK,)
    return pl.pallas_call(
        handoff_kernel,
        out_shape=shape(dims, bf16),
        compiler_params=params(16),
        cost_estimate=cost(1),
        name="handoff",
    )(terms)


def prefix_terms(t, kt, d, rows):
    key_heads, blocks = t.shape[0], t.shape[1]
    each = heads_at_once(key_heads, PREFIX_STEP)

    def some(dims):
        return pl.BlockSpec((each,) + dims, lambda p: (p,) + (0,) * len(dims))

    outs = [(blocks, SHARE, CH, DK), (blocks - 1, SHARE, DK, DK)]
    return pl.pallas_call(
        prefix_kernel,
        grid=(key_heads // each,),
        in_specs=[some(x.shape[1:]) for x in (t, kt, d, rows)],
        out_specs=[some(dims) for dims in outs],
        out_shape=[shape((key_heads,) + dims, bf16) for dims in outs],
        compiler_params=params(),
        cost_estimate=cost(5),
        name="prefix_terms",
    )(t, kt, d, rows)


def normed_rows(member, terms, state, gate, gain, parity):
    heads = state.shape[0]
    count = len(gate)
    size, width = gate[0].shape

    def token_block(i):
        return pl.BlockSpec(
            (heads, size, DK + DV), lambda p, me: (0, me[0] ^ (2 * i + parity), 0)
        )

    whole = pl.BlockSpec((size, width), lambda p, me: (0, 0))
    return pl.pallas_call(
        functools.partial(norm_kernel, count),
        grid_spec=grid_of(
            1,
            [token_block(i) for i in range(count)]
            + [whole] * count
            + [
                pl.BlockSpec((heads, DK, DV), lambda p, me: (0, 0, 0)),
                pl.BlockSpec((1, DV), lambda p, me: (0, 0)),
            ],
            pl.BlockSpec((count, size, width), lambda p, me: (0, 0, 0)),
            [],
        ),
        out_shape=shape((count, size, width), bf16),
        compiler_params=params(16),
        cost_estimate=cost(1),
        name="normed_rows",
    )(member, *([terms] * count), *gate, state, gain)


def projected(mine, theirs, own_weight, other_weight, start, width):
    ranks, size, depth = mine.shape
    tile = min(width, 512)
    whole = pl.BlockSpec((ranks, size, depth), lambda j: (0, 0, 0))
    weight = pl.BlockSpec((depth, tile), lambda j: (0, j + start // tile))
    out = pl.BlockSpec((size, tile), lambda j: (0, j))
    return pl.pallas_call(
        project_kernel,
        grid=(width // tile,),
        in_specs=[whole, whole, weight, weight],
        out_specs=[out] * ranks,
        out_shape=[shape((size, width), f32)] + [shape((size, width), bf16)] * (ranks - 1),
        compiler_params=params(16),
        cost_estimate=cost(3),
        name="projected",
    )(mine, theirs, own_weight, other_weight)


def sum_kernel(cuts, *refs):
    parts, out = refs[:-1], refs[-1]
    each = len(parts) // cuts
    for cut in range(cuts):
        total = parts[cut * each][...]
        for part in parts[cut * each + 1 : (cut + 1) * each]:
            total = total + part[...].astype(f32)
        width = total.shape[1]
        out[:, cut * width : (cut + 1) * width] = total.astype(bf16)


def summed_parts(parts, cuts):
    rows, width = parts[0].shape
    return pl.pallas_call(
        functools.partial(sum_kernel, cuts),
        out_shape=shape((rows, width * cuts), bf16),
        compiler_params=params(16),
        cost_estimate=cost(1),
        name="summed_parts",
    )(*parts)


def to_members(pieces):
    groups = len(pieces)
    return [pieces[0]] + [
        lax.ppermute(pieces[d], "head", [(i, i ^ d) for i in range(groups)])
        for d in range(1, groups)
    ]


def after_all(values, others):
    return lax.optimization_barrier((*values, *others))[: len(values)]


def to_runners(terms):
    spans = lax.axis_size("seq")
    heads = terms.shape[0]
    if spans <= heads:
        pieces = terms.reshape(spans, heads // spans, DK, DK + DV)
    else:
        cuts = spans // heads
        maps = jnp.repeat(terms[:, :, :DK], cuts, axis=0)
        adds = terms[:, :, DK:].reshape(heads, DK, cuts, DV // cuts)
        adds = adds.transpose(0, 2, 1, 3).reshape(spans, DK, DV // cuts)
        pieces = jnp.concatenate([maps, adds], axis=2)[:, None]
    return lax.all_to_all(pieces, "seq", 0, 0)


def from_runners(entries, heads):
    spans, each, depth, width = entries.shape
    entries = lax.all_to_all(entries, "seq", 0, 0)
    entries = entries.reshape(heads // each, DV // width, each, depth, width)
    return entries.transpose(0, 2, 3, 1, 4).reshape(heads, depth, DV)


def on_device(
    query_input,
    key_input,
    value_input,
    gate_input,
    write_strength,
    log_decay,
    filter_query,
    filter_key,
    filter_value,
    norm_gain,
    out_weight,
):
    groups = lax.axis_size("head")
    spans = lax.axis_size("seq")
    member = lax.axis_index("head").astype(jnp.int32).reshape(1)
    heads = filter_value.shape[1] // DV

    key_out = pack_keys(
        member, key_input, value_input, query_input, write_strength.T, log_decay.T, groups
    )
    packed = to_members(key_out)
    edge = packed[0][-2 * EDGE :]
    for d in range(1, groups):
        edge = jnp.where((member[0] ^ d) == groups - 1, packed[d][-2 * EDGE :], edge)
    edge = jnp.where(lax.axis_index("seq") == spans - 1, jnp.zeros_like(edge), edge)
    value_out = pack(member, value_input, groups)
    query_out = pack(member, query_input, groups)
    gate_out = pack(member, gate_input, groups)
    edge, *value_out = after_all([edge, *value_out], [*query_out, *gate_out])
    edge = lax.ppermute(edge, "seq", [(s, (s + 1) % spans) for s in range(spans)])
    value_rows = to_members(value_out)
    t, kt, d, rows, maps = key_terms(member, packed, edge, filter_key)
    u, z, adds = value_terms(member, value_rows, edge, filter_value, t, kt, d, rows, maps)
    query_rows = to_members(after_all(query_out, [adds]))
    gate_rows = to_members(after_all(gate_out, [adds]))
    swap = [(i, i ^ 1) for i in range(groups)]
    (own_weight,) = after_all([out_weight], [adds])
    other_weight = lax.ppermute(own_weight, "head", swap)
    w, p = prefix_terms(*after_all([t, kt, d, rows], [adds]))
    adds, w, p = after_all([to_runners(adds), w, p], [])
    entries = handoff(adds)
    query_rows = after_all(query_rows, [entries, *gate_rows])
    terms = query_terms(member, query_rows, edge, packed, filter_query, kt, w, p, u, z)
    state = from_runners(entries, heads)

    gain = norm_gain.reshape(1, DV)
    theirs = normed_rows(member, terms, state, gate_rows[1::2], gain, 1)
    theirs = lax.ppermute(theirs, "head", swap)
    mine = normed_rows(member, terms, state, gate_rows[0::2], gain, 0)
    width = out_weight.shape[1]
    cuts = 2
    parts = []
    for cut in range(cuts):
        kept, *sent = projected(
            mine, theirs, out_weight, other_weight, cut * width // cuts, width // cuts
        )
        parts.append(kept)
        parts += [
            lax.ppermute(part, "head", [(i, i ^ (2 * step + 2)) for i in range(groups)])
            for step, part in enumerate(sent)
        ]
    return summed_parts(parts, cuts)


def solution(mesh):
    tokens = P(("seq", "head"), None)
    placed = (tokens,) * 6 + (P(None, "head"),) * 3 + (P(), P("head", None))
    return jax.shard_map(
        on_device, mesh=mesh, in_specs=placed, out_specs=tokens, check_vma=False
    )
```

```python
import functools

import jax
import jax.numpy as jnp
from jax import lax
from jax.experimental import pallas as pl
from jax.experimental.pallas import tpu as pltpu
from jax.sharding import PartitionSpec as P

HK = 16
HV = 32
DK = 128
DV = 128
CH = 128
EDGE = 16
SHARE = HV // HK
ANYWHERE = pl.BlockSpec(memory_space=pl.ANY)
ODD_ROWS = 16

norm_floor = 1e-06
f32 = jnp.float32
bf16 = jnp.bfloat16


def params(megabytes=60):
    return pltpu.CompilerParams(vmem_limit_bytes=megabytes * 1024 * 1024)


def split(x):
    high = x.astype(bf16)
    return high, (x - high.astype(f32)).astype(bf16)


def as_left(x):
    return jnp.concatenate(split(x), axis=1)


def right_of(high, low):
    row = jnp.concatenate([high, low], axis=1)
    return jnp.concatenate([row, row], axis=0)


def as_right(x):
    return right_of(*split(x))


def product(left, right):
    both = jnp.dot(left, right, preferred_element_type=f32)
    half = both.shape[1] // 2
    return both[:, :half] + both[:, half:]


def grids():
    row = lax.broadcasted_iota(jnp.int32, (CH, CH), 0)
    column = lax.broadcasted_iota(jnp.int32, (CH, CH), 1)
    return row, column


def ones_where(mask):
    return jnp.where(mask, 1.0, 0.0).astype(bf16)


def place(me, pieces, out, margin):
    size = pieces[0].shape[0]
    for d, piece in enumerate(pieces):
        at = pl.multiple_of((me ^ d) * size + margin, 8)
        out[pl.ds(at, size), :] = piece[...].astype(out.dtype)


def place_gates(me, pieces, out, heads, size):
    for d, piece in enumerate(pieces):
        ends = piece[...].astype(f32)[12:16]
        sets = [ends[:, i * size : (i + 1) * size] for i in range(heads // 2)]
        rows = jnp.concatenate(sets + [jnp.zeros((128 - 2 * heads, size), f32)], axis=0)
        at = pl.multiple_of((me ^ d) * size, 16)
        out[pl.ds(at, size), :] = jnp.transpose(rows).astype(bf16)


def conv_silu(me, pieces, edge, taps_ref, padded):
    length = padded.shape[0] - 8
    taps = taps_ref[...].astype(f32)
    padded[8 - edge.shape[0] : 8] = edge
    place(me, pieces, padded, 8)
    margin = taps.shape[0] - 1
    summed = taps[margin : margin + 1] * padded[8 : 8 + length]
    for offset in range(margin):
        start = 8 - margin + offset
        summed = summed + taps[offset : offset + 1] * padded[start : start + length]
    return summed / (1.0 + jnp.exp(-summed))


def unit_rows(field):
    return field * lax.rsqrt(jnp.sum(field * field, axis=-1, keepdims=True) + norm_floor)


def strengths_and_rates(gates, first, count, heads):
    lane = lax.broadcasted_iota(jnp.int32, (gates.shape[1], CH), 0)
    picks = [ones_where(lane == first + e) for e in range(count)]
    picks += [ones_where(lane == heads + first + e) for e in range(count)]
    picked = jnp.dot(gates, jnp.concatenate(picks, axis=1), preferred_element_type=f32)
    return picked[:, : count * CH], picked[:, count * CH :].astype(bf16)


def decay_terms(rates, count, with_growth=True):
    row, column = grids()
    below = ones_where(column <= row)
    pieces = []
    for e in range(count):
        rate = rates[:, e * CH : (e + 1) * CH]
        pieces.append(jnp.where(row > column, rate, jnp.zeros_like(rate)))
    if with_growth:
        pieces.append(rates)
    sums = jnp.dot(below, jnp.concatenate(pieces, axis=1), preferred_element_type=f32)
    ratios, growth = [], []
    for e in range(count):
        at = e * CH
        ratios.append(jnp.where(column <= row, jnp.exp(sums[:, at : at + CH]), 0.0))
        if with_growth:
            at += count * CH
            growth.append(jnp.exp(sums[:, at : at + CH]))
    return ratios, growth


def unit_lower_inverses(lower):
    row, column = grids()
    names = list(lower)
    eye = jnp.where(row == column, 1.0, 0.0)
    pair = (row // 2 == column // 2) & (column < row)
    halves = {n: split(lower[n]) for n in names}
    inverse = {n: eye - jnp.where(pair, lower[n], 0.0) for n in names}
    size = 2
    while size < CH:
        mask = ones_where(
            (row // (2 * size) == column // (2 * size))
            & ((row // size) % 2 == 1)
            & ((column // size) % 2 == 0)
        )
        rounded = {n: inverse[n].astype(bf16) for n in names}
        if size < ODD_ROWS:
            first = {
                n: jnp.dot(halves[n][0] * mask, rounded[n], preferred_element_type=f32).astype(bf16)
                for n in names
            }
            for n in names:
                inverse[n] = inverse[n] - jnp.dot(rounded[n], first[n], preferred_element_type=f32)
        else:
            starts = range(size, CH, 2 * size)

            def odd(x):
                return jnp.concatenate([x[s : s + size] for s in starts], axis=0)

            def back(x, even):
                rows = []
                for i, s in enumerate(starts):
                    rows += [even[s - size : s], x[i * size : (i + 1) * size]]
                return jnp.concatenate(rows, axis=0)

            some = odd(mask)
            nothing = jnp.zeros((CH, CH), bf16)
            first = {
                n: jnp.dot(
                    odd(halves[n][0]) * some, rounded[n], preferred_element_type=f32
                ).astype(bf16)
                for n in names
            }
            for n in names:
                change = jnp.dot(
                    odd(rounded[n]), back(first[n], nothing), preferred_element_type=f32
                )
                inverse[n] = back(odd(inverse[n]) - change, inverse[n])
        size *= 2
    parts = {n: split(inverse[n]) for n in names}
    left = {
        n: (
            eye
            - inverse[n]
            - product(jnp.concatenate(halves[n], axis=1), right_of(*parts[n]))
        ).astype(bf16)
        for n in names
    }
    return {
        n: inverse[n] + jnp.dot(parts[n][0], left[n], preferred_element_type=f32) for n in names
    }


def key_kernel(groups_count, heads, member, *refs):
    pieces, refs = refs[:groups_count], refs[groups_count:]
    gate_pieces, refs = refs[:groups_count], refs[groups_count:]
    edge, taps, t_out, kt_out, d_out, rows_out, map_out, padded, gates = refs
    here = pieces[0].shape[1] // DK
    count = here * SHARE
    blocks = gates.shape[0] // CH
    me = member[0]
    first = pl.program_id(0) * count
    filtered = conv_silu(me, pieces, edge[...].astype(f32)[EDGE - 8 :], taps, padded)
    place_gates(me, gate_pieces, gates, heads, pieces[0].shape[0])
    row, column = grids()
    eye = jnp.where(row == column, 1.0, 0.0)
    groups = [(c, k) for c in range(blocks) for k in range(here)]
    problems = [(c, e) for c in range(blocks) for e in range(count)]

    def chunk_of(x, c):
        return x[c * CH : (c + 1) * CH]

    strengths, rates = strengths_and_rates(gates[...], first, count, heads)
    unit = [unit_rows(filtered[:, k * DK : (k + 1) * DK]) for k in range(here)]
    ratio = [decay_terms(chunk_of(rates, c), count, False)[0] for c in range(blocks)]
    keys = {(c, k): chunk_of(unit[k], c) for c, k in groups}
    turned = {g: jnp.transpose(keys[g]) for g in groups}
    sides = {g: split(turned[g]) for g in groups}
    kk = {g: product(as_left(keys[g]), right_of(*sides[g])) for g in groups}
    lane = lax.broadcasted_iota(jnp.int32, (2 * count, gates.shape[1]), 1)
    order = lax.broadcasted_iota(jnp.int32, (2 * count, gates.shape[1]), 0)
    pick = ones_where(lane == first + jnp.where(order < count, order, order - count + heads))
    across = [
        lax.dot_general(
            pick,
            gates[c * CH : (c + 1) * CH, :],
            (((1,), (1,)), ((), ())),
            preferred_element_type=f32,
        )
        for c in range(blocks)
    ]
    growing = [
        jnp.exp(
            jnp.dot(across[c].astype(bf16), ones_where(row <= column), preferred_element_type=f32)
        )
        for c in range(blocks)
    ]
    lower, ktail, ends = {}, {}, {}
    for c, k in groups:
        kt_out[k, c] = jnp.concatenate(sides[c, k], axis=1)
    for c, e in problems:
        ratios = ratio[c][e]
        strength = chunk_of(strengths, c)[:, e * CH : (e + 1) * CH]
        k = e // SHARE
        lower[c, e] = jnp.where(column < row, strength * kk[c, k] * ratios, 0.0)
        ktail[c, e] = (turned[c, k] * ratios[CH - 1 : CH]).astype(bf16)
        growth = growing[c][count + e : count + e + 1]
        ends[c, e] = jnp.broadcast_to(growth[:, CH - 1 : CH], (1, CH))
        rows_out[k, c, e % SHARE] = jnp.concatenate(
            [ratios[CH - 1 : CH], growth] + [ends[c, e]] * 6, axis=0
        )
    inverse = unit_lower_inverses(lower)
    solving = {
        (c, e): (inverse[c, e] * across[c][e : e + 1]).astype(bf16) for c, e in problems
    }
    rounded = {g: keys[g].astype(bf16) for g in groups}
    solved = {
        (c, e): jnp.dot(
            (
                inverse[c, e]
                * (across[c][e : e + 1] * growing[c][count + e : count + e + 1])
            ).astype(bf16),
            rounded[c, e // SHARE],
            preferred_element_type=f32,
        ).astype(bf16)
        for c, e in problems
    }
    maps = {
        pc: jnp.dot(ktail[pc], solved[pc], preferred_element_type=f32).astype(bf16)
        for pc in problems
    }
    for c, e in problems:
        k = e // SHARE
        t_out[k, c, e % SHARE] = solving[c, e]
        d_out[k, c, e % SHARE] = maps[c, e]
    running = [
        ends[0, e] * eye - maps[0, e].astype(f32) for e in range(count)
    ]
    for c in range(1, blocks):
        running = [
            ends[c, e] * running[e]
            - jnp.dot(maps[c, e], running[e].astype(bf16), preferred_element_type=f32)
            for e in range(count)
        ]
    for e in range(count):
        map_out[e] = (eye - running[e]).astype(bf16)


def prefix_kernel(t_in, kt_in, d_in, rows_in, w_out, p_out):
    here, blocks = t_in.shape[0], t_in.shape[1]
    count = here * SHARE
    row, column = grids()
    eye = jnp.where(row == column, 1.0, 0.0)

    def at(ref, c, e):
        return ref[e // SHARE, c, e % SHARE]

    keys = {
        (c, k): jnp.transpose(whole_of(kt_in[k, c])).astype(bf16)
        for c in range(blocks)
        for k in range(here)
    }
    problems = [(c, e) for c in range(blocks) for e in range(count)]
    scaled = {
        (c, e): (at(t_in, c, e).astype(f32) * at(rows_in, c, e)[1:2]).astype(bf16) for c, e in problems
    }
    for c, e in problems:
        solved = jnp.dot(scaled[c, e], keys[c, e // SHARE], preferred_element_type=f32)
        w_out[e // SHARE, c, e % SHARE] = solved.astype(bf16)
    running = [
        at(rows_in, 0, e)[7:8] * eye - at(d_in, 0, e).astype(f32) for e in range(count)
    ]
    for c in range(1, blocks):
        parts = [x.astype(bf16) for x in running]
        for e in range(count):
            p_out[e // SHARE, c - 1, e % SHARE] = parts[e]
        if c + 1 < blocks:
            running = [
                at(rows_in, c, e)[7:8] * running[e]
                - jnp.dot(at(d_in, c, e), parts[e], preferred_element_type=f32)
                for e in range(count)
            ]


def both_of(left, parts):
    both = jnp.dot(left, jnp.concatenate(parts, axis=1), preferred_element_type=f32)
    half = both.shape[1] // 2
    return both[:, :half] + both[:, half:]


def whole_of(both):
    half = both.shape[1] // 2
    return both[:, :half].astype(f32) + both[:, half:].astype(f32)


def right_from(both):
    return jnp.concatenate([both, both], axis=0)


def value_kernel(groups_count, member, *refs):
    pieces, refs = refs[:groups_count], refs[groups_count:]
    edge, taps, t_in, kt_in, d_in, rows_in, maps, u_out, z_out, span_out, padded, before = refs
    blocks = t_in.shape[1]
    width = pieces[0].shape[1]
    count = width // DV
    ends = edge[...].astype(f32)
    for r in range(SHARE):
        before[:, r * edge.shape[1] : (r + 1) * edge.shape[1]] = ends[4 * r : 4 * r + 4]
    at = pl.multiple_of(pl.program_id(0) * width, 128)
    values = conv_silu(member[0], pieces, before[:, pl.ds(at, width)], taps, padded)
    problems = [(c, e) for c in range(blocks) for e in range(count)]

    def at(ref, c, e):
        return ref[e // SHARE, c, e % SHARE]

    written = {
        (c, e): split(
            jnp.dot(
                at(t_in, c, e),
                values[c * CH : (c + 1) * CH, e * DV : (e + 1) * DV].astype(bf16),
                preferred_element_type=f32,
            )
        )
        for c, e in problems
    }
    tailed = {
        (c, e): (whole_of(kt_in[e // SHARE, c]) * at(rows_in, c, e)[0:1]).astype(bf16)
        for c, e in problems
    }
    adds = {
        pc: jnp.dot(tailed[pc], written[pc][0], preferred_element_type=f32) for pc in problems
    }
    for c, e in problems:
        u_out[e // SHARE, c, e % SHARE] = jnp.concatenate(written[c, e], axis=1)
    running = [adds[0, e] for e in range(count)]
    for c in range(1, blocks):
        parts = [x.astype(bf16) for x in running]
        for e in range(count):
            z_out[e // SHARE, c - 1, e % SHARE] = parts[e]
        running = [
            at(rows_in, c, e)[7:8] * running[e]
            - jnp.dot(at(d_in, c, e), parts[e], preferred_element_type=f32)
            + adds[c, e]
            for e in range(count)
        ]
    for e in range(count):
        span_out[e, :, :DK] = maps[e]
        span_out[e, :, DK:] = running[e].astype(bf16)


def query_kernel(groups_count, heads, member, *refs):
    pieces, refs = refs[:groups_count], refs[groups_count:]
    gate_pieces, refs = refs[:groups_count], refs[groups_count:]
    edge, taps, kt_in, w_in, p_in, u_in, z_in, out, padded, gates = refs
    here = pieces[0].shape[1] // DK
    count = here * SHARE
    blocks = gates.shape[0] // CH
    me = member[0]
    first = pl.program_id(0) * count
    filtered = conv_silu(me, pieces, edge[...].astype(f32)[8:12], taps, padded)
    place_gates(me, gate_pieces, gates, heads, pieces[0].shape[0])
    unit = [unit_rows(filtered[:, k * DK : (k + 1) * DK]) * DK ** (-0.5) for k in range(here)]
    problems = [(c, e) for c in range(blocks) for e in range(count)]
    strengths, rates = strengths_and_rates(gates[...], first, count, heads)
    decays = [decay_terms(rates[c * CH : (c + 1) * CH], count) for c in range(blocks)]

    def at(ref, c, e):
        return right_from(ref[e // SHARE, c, e % SHARE])

    queries = {
        (c, k): unit[k][c * CH : (c + 1) * CH] for c in range(blocks) for k in range(here)
    }
    qk = {
        (c, k): product(as_left(queries[c, k]), right_from(kt_in[k, c])) for c, k in queries
    }
    mix = {(c, e): as_left(qk[c, e // SHARE] * decays[c][0][e]) for c, e in problems}
    entry = {
        (c, e): as_left(
            decays[c][1][e] * queries[c, e // SHARE]
            - jnp.dot(mix[c, e], at(w_in, c, e), preferred_element_type=f32)
        )
        for c, e in problems
    }
    local = {pc: product(mix[pc], at(u_in, *pc)) for pc in problems}
    for c, e in problems:
        here = slice(c * CH, (c + 1) * CH)
        if c == 0:
            out[e, here, :DK] = entry[c, e][:, :DK]
            out[e, here, DK:] = local[c, e].astype(bf16)
        else:
            out[e, here, :DK] = jnp.dot(
                entry[c, e], at(p_in, c - 1, e), preferred_element_type=f32
            ).astype(bf16)
            later = jnp.dot(entry[c, e], at(z_in, c - 1, e), preferred_element_type=f32)
            out[e, here, DK:] = (local[c, e] + later).astype(bf16)


def handoff_kernel(terms, out):
    spans, heads, width = out.shape[0], out.shape[1], out.shape[3]
    running = [jnp.zeros(out.shape[2:], f32) for h in range(heads)]
    for j in range(spans):
        for h in range(heads):
            out[j, h] = running[h].astype(bf16)
        if j + 1 < spans:
            for h in range(heads):
                erased = jnp.dot(
                    terms[j, h, :, :DK],
                    jnp.concatenate(split(running[h]), axis=1),
                    preferred_element_type=f32,
                )
                erased = erased[:, :width] + erased[:, width:]
                running[h] = running[h] - erased + terms[j, h, :, DK:].astype(f32)


def norm_kernel(count, member, *refs):
    terms, refs = refs[:count], refs[count:]
    gate, refs = refs[:count], refs[count:]
    state, gain, out = refs
    cells = [(i, h) for i in range(count) for h in range(state.shape[0])]
    core = {
        (i, h): terms[i][h, :, DK:].astype(f32)
        + jnp.dot(terms[i][h, :, :DK], state[h], preferred_element_type=f32)
        for i, h in cells
    }
    scale = {
        n: lax.rsqrt(jnp.mean(core[n] * core[n], axis=-1, keepdims=True) + norm_floor)
        for n in cells
    }
    for i, h in cells:
        columns = slice(h * DV, (h + 1) * DV)
        gates = gate[i][:, columns].astype(f32)
        gates = gates / (1.0 + jnp.exp(-gates))
        out[i, :, columns] = (core[i, h] * scale[i, h] * gain[...] * gates).astype(bf16)


def project_kernel(mine, theirs, own_weight, other_weight, kept, *sent):
    rows, depth = mine.shape[0] * mine.shape[1], mine.shape[2]
    product_ = jnp.dot(
        mine[...].reshape(rows, depth), own_weight[...], preferred_element_type=f32
    ) + jnp.dot(theirs[...].reshape(rows, depth), other_weight[...], preferred_element_type=f32)
    size = mine.shape[1]
    kept[...] = product_[:size]
    for i, out in enumerate(sent):
        out[...] = product_[(i + 1) * size : (i + 2) * size].astype(bf16)


def pack_kernel(groups_count, member, *refs):
    array, outs = refs[0], refs[1:]
    me = member[0]
    width = array.shape[1] // groups_count
    for d in range(groups_count):
        at = pl.multiple_of((me ^ d) * width, 128)
        outs[d][...] = array[:, pl.ds(at, width)]


def pack_keys_kernel(groups_count, member, *refs):
    key, value_end, query_end, strength, decay = refs[:5]
    outs = refs[5:]
    me = member[0]
    tokens, width = key.shape[0], key.shape[1] // groups_count
    heads = HV // groups_count
    gates = jnp.concatenate([strength[...], decay[...]], axis=0)
    row = lax.broadcasted_iota(jnp.int32, (2 * heads, 2 * HV), 0)
    column = lax.broadcasted_iota(jnp.int32, (2 * heads, 2 * HV), 1)
    for d in range(groups_count):
        at = me ^ d
        outs[d][:tokens] = key[:, pl.ds(pl.multiple_of(at * width, 128), width)]
        ends = []
        for r in range(SHARE):
            start = pl.multiple_of((at * SHARE + r) * width, 128)
            ends.append(value_end[:, pl.ds(start, width)].astype(f32)[EDGE - 4 :])
        start = pl.multiple_of(at * width, 128)
        ends.append(query_end[:, pl.ds(start, width)].astype(f32)[EDGE - 4 :])
        wanted = jnp.where(row < heads, row, row - heads + HV) + at * heads
        picked = jnp.dot(ones_where(column == wanted), gates, preferred_element_type=f32)
        sets = [picked[4 * i : 4 * i + 4] for i in range(heads // 2)]
        if width > tokens * len(sets):
            sets.append(jnp.zeros((4, width - tokens * len(sets)), f32))
        ends.append(jnp.concatenate(sets, axis=1))
        outs[d][tokens:] = jnp.concatenate(ends, axis=0).astype(bf16)


def shape(dims, kind):
    return jax.ShapeDtypeStruct(dims, kind)


def pack(member, array, groups):
    tokens, width = array.shape[0], array.shape[1] // groups
    return pl.pallas_call(
        functools.partial(pack_kernel, groups),
        grid_spec=grid_of(
            1,
            [pl.BlockSpec(array.shape, lambda p, me: (0, 0))],
            [pl.BlockSpec((tokens, width), lambda p, me: (0, 0))] * groups,
            [],
        ),
        out_shape=[shape((tokens, width), bf16)] * groups,
        compiler_params=params(),
        cost_estimate=cost(3),
        name="pack",
    )(member, array)


def pack_keys(member, key, value, query, strength, decay, groups):
    tokens, width = key.shape[0], key.shape[1] // groups

    def whole(dims):
        return pl.BlockSpec(dims, lambda p, me: (0, 0))

    def end(x):
        return pl.BlockSpec((EDGE, x.shape[1]), lambda p, me: (tokens // EDGE - 1, 0))

    packed = (tokens + EDGE, width)
    return pl.pallas_call(
        functools.partial(pack_keys_kernel, groups),
        grid_spec=grid_of(
            1,
            [whole(key.shape), end(value), end(query), whole(strength.shape), whole(decay.shape)],
            [whole(packed)] * groups,
            [],
        ),
        out_shape=[shape(packed, bf16)] * groups,
        compiler_params=params(),
        cost_estimate=cost(3),
        name="pack_keys",
    )(member, key, value, query, strength, decay)


def per_head(each, dims):
    return pl.BlockSpec((each,) + dims, lambda p, me: (p,) + (0,) * len(dims))


def columns_of(rows, width):
    return pl.BlockSpec((rows, width), lambda p, me: (0, p))


KEY_STEP, VALUE_STEP, PREFIX_STEP, QUERY_STEP = 2, 2, 2, 2


def heads_at_once(key_heads, most):
    return most if key_heads % most == 0 else key_heads


def cost(microseconds):
    return pl.CostEstimate(
        flops=int(microseconds * 1e9), bytes_accessed=int(microseconds * 3e6), transcendentals=0
    )


def grid_of(steps, in_specs, out_specs, scratch):
    return pltpu.PrefetchScalarGridSpec(
        num_scalar_prefetch=1,
        grid=(steps,),
        in_specs=in_specs,
        out_specs=out_specs,
        scratch_shapes=scratch,
    )


def key_terms(member, packed, edge, taps):
    groups = len(packed)
    own = packed[0].shape[0] - EDGE
    tokens = groups * own
    key_heads = taps.shape[1] // DK
    each = heads_at_once(key_heads, KEY_STEP)
    blocks = tokens // CH
    wide = (blocks, SHARE, CH, 2 * CH)
    kinds = [
        (blocks, SHARE, CH, CH),
        (blocks, DK, 2 * CH),
        (blocks, SHARE, DK, DK),
        (blocks, SHARE, 8, CH),
    ]
    types = [bf16] * 3 + [f32]
    return pl.pallas_call(
        functools.partial(key_kernel, groups, key_heads * SHARE),
        grid_spec=grid_of(
            key_heads // each,
            [columns_of(own, each * DK)] * groups
            + [pl.BlockSpec((EDGE, key_heads * DK), lambda p, me: (own // EDGE, 0))] * groups
            + [columns_of(EDGE, each * DK)]
            + [columns_of(taps.shape[0], each * DK)],
            [per_head(each, kind) for kind in kinds]
            + [pl.BlockSpec((each * SHARE, DK, DK), lambda p, me: (p, 0, 0))],
            [pltpu.VMEM((tokens + 8, each * DK), f32), pltpu.VMEM((tokens, 128), bf16)],
        ),
        out_shape=[shape((key_heads,) + kind, t) for kind, t in zip(kinds, types)]
        + [shape((key_heads * SHARE, DK, DK), bf16)],
        compiler_params=params(),
        cost_estimate=cost(12),
        name="key_terms",
    )(member, *packed, *packed, edge, taps)


def value_terms(member, pieces, edge, taps, t_in, kt_in, d_in, rows_in, maps):
    groups = len(pieces)
    own = pieces[0].shape[0]
    tokens = groups * own
    key_heads = t_in.shape[0]
    each = heads_at_once(key_heads, VALUE_STEP)
    blocks = tokens // CH
    width = each * SHARE * DV
    return pl.pallas_call(
        functools.partial(value_kernel, groups),
        grid_spec=grid_of(
            key_heads // each,
            [columns_of(own, width)] * groups
            + [pl.BlockSpec((EDGE, key_heads * DK), lambda p, me: (1, 0))]
            + [columns_of(taps.shape[0], width)]
            + [per_head(each, x.shape[1:]) for x in (t_in, kt_in, d_in, rows_in)]
            + [pl.BlockSpec((each * SHARE, DK, DK), lambda p, me: (p, 0, 0))],
            [
                per_head(each, (blocks, SHARE, CH, 2 * DV)),
                per_head(each, (blocks - 1, SHARE, DK, DV)),
                pl.BlockSpec((each * SHARE, DK, DK + DV), lambda p, me: (p, 0, 0)),
            ],
            [
                pltpu.VMEM((tokens + 8, width), f32),
                pltpu.VMEM((4, key_heads * SHARE * DV), f32),
            ],
        ),
        out_shape=[
            shape((key_heads, blocks, SHARE, CH, 2 * DV), bf16),
            shape((key_heads, blocks - 1, SHARE, DK, DV), bf16),
            shape((key_heads * SHARE, DK, DK + DV), bf16),
        ],
        compiler_params=params(),
        cost_estimate=cost(7),
        name="value_terms",
    )(member, *pieces, edge, taps, t_in, kt_in, d_in, rows_in, maps)


def query_terms(member, pieces, edge, packed, taps, kt, w, p, u, z):
    groups = len(pieces)
    own = pieces[0].shape[0]
    tokens = groups * own
    key_heads = kt.shape[0]
    each = heads_at_once(key_heads, QUERY_STEP)
    out = pl.BlockSpec((each * SHARE, tokens, DK + DV), lambda p, me: (p, 0, 0))
    return pl.pallas_call(
        functools.partial(query_kernel, groups, key_heads * SHARE),
        grid_spec=grid_of(
            key_heads // each,
            [columns_of(own, each * DK)] * groups
            + [pl.BlockSpec((EDGE, key_heads * DK), lambda p, me: (own // EDGE, 0))] * groups
            + [pl.BlockSpec((EDGE, each * DK), lambda p, me: (1, p))]
            + [columns_of(taps.shape[0], each * DK)]
            + [per_head(each, x.shape[1:]) for x in (kt, w, p, u, z)],
            out,
            [pltpu.VMEM((tokens + 8, each * DK), f32), pltpu.VMEM((tokens, 128), bf16)],
        ),
        out_shape=shape((key_heads * SHARE, tokens, DK + DV), bf16),
        compiler_params=params(),
        cost_estimate=cost(9),
        name="query_terms",
    )(member, *pieces, *packed, edge, taps, kt, w, p, u, z)


def handoff(terms):
    dims = terms.shape[:3] + (terms.shape[3] - DK,)
    return pl.pallas_call(
        handoff_kernel,
        out_shape=shape(dims, bf16),
        compiler_params=params(16),
        cost_estimate=cost(1),
        name="handoff",
    )(terms)


def prefix_terms(t, kt, d, rows):
    key_heads, blocks = t.shape[0], t.shape[1]
    each = heads_at_once(key_heads, PREFIX_STEP)

    def some(dims):
        return pl.BlockSpec((each,) + dims, lambda p: (p,) + (0,) * len(dims))

    outs = [(blocks, SHARE, CH, DK), (blocks - 1, SHARE, DK, DK)]
    return pl.pallas_call(
        prefix_kernel,
        grid=(key_heads // each,),
        in_specs=[some(x.shape[1:]) for x in (t, kt, d, rows)],
        out_specs=[some(dims) for dims in outs],
        out_shape=[shape((key_heads,) + dims, bf16) for dims in outs],
        compiler_params=params(),
        cost_estimate=cost(5),
        name="prefix_terms",
    )(t, kt, d, rows)


def normed_rows(member, terms, state, gate, gain, parity):
    heads = state.shape[0]
    count = len(gate)
    size, width = gate[0].shape

    def token_block(i):
        return pl.BlockSpec(
            (heads, size, DK + DV), lambda p, me: (0, me[0] ^ (2 * i + parity), 0)
        )

    whole = pl.BlockSpec((size, width), lambda p, me: (0, 0))
    return pl.pallas_call(
        functools.partial(norm_kernel, count),
        grid_spec=grid_of(
            1,
            [token_block(i) for i in range(count)]
            + [whole] * count
            + [
                pl.BlockSpec((heads, DK, DV), lambda p, me: (0, 0, 0)),
                pl.BlockSpec((1, DV), lambda p, me: (0, 0)),
            ],
            pl.BlockSpec((count, size, width), lambda p, me: (0, 0, 0)),
            [],
        ),
        out_shape=shape((count, size, width), bf16),
        compiler_params=params(16),
        cost_estimate=cost(1),
        name="normed_rows",
    )(member, *([terms] * count), *gate, state, gain)


def projected(mine, theirs, own_weight, other_weight, start, width):
    ranks, size, depth = mine.shape
    tile = min(width, 512)
    whole = pl.BlockSpec((ranks, size, depth), lambda j: (0, 0, 0))
    weight = pl.BlockSpec((depth, tile), lambda j: (0, j + start // tile))
    out = pl.BlockSpec((size, tile), lambda j: (0, j))
    return pl.pallas_call(
        project_kernel,
        grid=(width // tile,),
        in_specs=[whole, whole, weight, weight],
        out_specs=[out] * ranks,
        out_shape=[shape((size, width), f32)] + [shape((size, width), bf16)] * (ranks - 1),
        compiler_params=params(16),
        cost_estimate=cost(3),
        name="projected",
    )(mine, theirs, own_weight, other_weight)


def sum_kernel(count, *refs):
    parts, out = refs[:count], refs[-1]
    total = parts[0][...]
    for part in parts[1:]:
        total = total + part[...].astype(f32)
    out[...] = total.astype(bf16)


def summed_parts(parts, before, cut, cuts):
    rows, width = parts[0].shape
    whole = pl.BlockSpec((rows, width), lambda p: (0, 0))
    more = [] if before is None else [before]
    return pl.pallas_call(
        functools.partial(sum_kernel, len(parts)),
        grid=(1,),
        in_specs=[whole] * len(parts) + [ANYWHERE] * len(more),
        out_specs=pl.BlockSpec((rows, width), lambda p: (0, cut)),
        out_shape=shape((rows, width * cuts), bf16),
        input_output_aliases={len(parts): 0} if more else {},
        compiler_params=params(16),
        cost_estimate=cost(1),
        name="summed_parts",
    )(*parts, *more)


def to_members(pieces):
    groups = len(pieces)
    return [pieces[0]] + [
        lax.ppermute(pieces[d], "head", [(i, i ^ d) for i in range(groups)])
        for d in range(1, groups)
    ]


def after_all(values, others):
    return lax.optimization_barrier((*values, *others))[: len(values)]


def to_runners(terms):
    spans = lax.axis_size("seq")
    heads = terms.shape[0]
    if spans <= heads:
        pieces = terms.reshape(spans, heads // spans, DK, DK + DV)
    else:
        cuts = spans // heads
        maps = jnp.repeat(terms[:, :, :DK], cuts, axis=0)
        adds = terms[:, :, DK:].reshape(heads, DK, cuts, DV // cuts)
        adds = adds.transpose(0, 2, 1, 3).reshape(spans, DK, DV // cuts)
        pieces = jnp.concatenate([maps, adds], axis=2)[:, None]
    return lax.all_to_all(pieces, "seq", 0, 0)


def from_runners(entries, heads):
    spans, each, depth, width = entries.shape
    entries = lax.all_to_all(entries, "seq", 0, 0)
    entries = entries.reshape(heads // each, DV // width, each, depth, width)
    return entries.transpose(0, 2, 3, 1, 4).reshape(heads, depth, DV)


def on_device(
    query_input,
    key_input,
    value_input,
    gate_input,
    write_strength,
    log_decay,
    filter_query,
    filter_key,
    filter_value,
    norm_gain,
    out_weight,
):
    groups = lax.axis_size("head")
    spans = lax.axis_size("seq")
    member = lax.axis_index("head").astype(jnp.int32).reshape(1)
    heads = filter_value.shape[1] // DV

    key_out = pack_keys(
        member, key_input, value_input, query_input, write_strength.T, log_decay.T, groups
    )
    packed = to_members(key_out)
    edge = packed[0][-2 * EDGE :]
    for d in range(1, groups):
        edge = jnp.where((member[0] ^ d) == groups - 1, packed[d][-2 * EDGE :], edge)
    edge = jnp.where(lax.axis_index("seq") == spans - 1, jnp.zeros_like(edge), edge)
    value_out = pack(member, value_input, groups)
    query_out = pack(member, query_input, groups)
    gate_out = pack(member, gate_input, groups)
    edge, *value_out = after_all([edge, *value_out], [*query_out, *gate_out])
    edge = lax.ppermute(edge, "seq", [(s, (s + 1) % spans) for s in range(spans)])
    value_rows = to_members(value_out)
    t, kt, d, rows, maps = key_terms(member, packed, edge, filter_key)
    u, z, adds = value_terms(member, value_rows, edge, filter_value, t, kt, d, rows, maps)
    query_rows = to_members(after_all(query_out, [adds]))
    gate_rows = to_members(after_all(gate_out, [adds]))
    swap = [(i, i ^ 1) for i in range(groups)]
    (own_weight,) = after_all([out_weight], [adds])
    other_weight = lax.ppermute(own_weight, "head", swap)
    w, p = prefix_terms(*after_all([t, kt, d, rows], [adds]))
    adds, w, p = after_all([to_runners(adds), w, p], [])
    entries = handoff(adds)
    query_rows = after_all(query_rows, [entries, *gate_rows])
    terms = query_terms(member, query_rows, edge, packed, filter_query, kt, w, p, u, z)
    state = from_runners(entries, heads)

    gain = norm_gain.reshape(1, DV)
    theirs = normed_rows(member, terms, state, gate_rows[1::2], gain, 1)
    theirs = lax.ppermute(theirs, "head", swap)
    mine = normed_rows(member, terms, state, gate_rows[0::2], gain, 0)
    width = out_weight.shape[1]
    cuts = 2
    parts = []
    for cut in range(cuts):
        kept, *sent = projected(
            mine, theirs, out_weight, other_weight, cut * width // cuts, width // cuts
        )
        parts.append([kept] + [
            lax.ppermute(part, "head", [(i, i ^ (2 * step + 2)) for i in range(groups)])
            for step, part in enumerate(sent)
        ])
    total = None
    for cut in range(cuts):
        total = summed_parts(parts[cut], total, cut, cuts)
    return total


def solution(mesh):
    tokens = P(("seq", "head"), None)
    placed = (tokens,) * 6 + (P(None, "head"),) * 3 + (P(), P("head", None))
    return jax.shard_map(
        on_device, mesh=mesh, in_specs=placed, out_specs=tokens, check_vma=False
    )
```
